256 devices in a mesh: gy: 32 (over y, z), gz: 8 (over x, core).
Axes of the slice: x: 4, y: 4, z: 8, core: 2. Of those that a mesh axis runs over, the one named last changes fastest.
Arguments:
- fields: float32 [2048, 4, 256, 128], P('gy', None, 'gz'), may hold values from -6 to 6
- kappa: float32 [2048, 256, 128], P('gy', 'gz'), may hold values from 0.02 to 0.16
- forward_mult: float32 [2048, 4], P('gy'), may hold values from 0.995 to 0.999
- pivot_inv: float32 [2048, 4], P('gy'), may hold values from 0.0001 to 0.001
- backward_mult: float32 [2048, 4], P('gy'), may hold values from 0.995 to 0.999
Outputs:
- solved: float32 [2048, 4, 256, 128], P('gy', None, 'gz')
The draws below stay inside these ranges and needn't reach their ends.
All inputs are finite; a program needn't handle non-finite values.
Results may differ from the reference program's by a relative error of at most 0.00021.
Values sent between devices are 32-bit elements; how exact they have to be, the bound alone decides.
No kernel may reach another device: no remote copies, remote signals or barrier semaphores. Data moves between devices by JAX's collectives and lax.ppermute only.
A program may use at most 128 MiB of HBM per device.

```python
import math
import jax
import jax.numpy as jnp
from jax import lax

FIELDS = 4
NX = 128
NY = 2048
NZ = 256


def draw_forward_mult(key, part):
    key = jax.random.fold_in(key, 11)
    return jax.random.uniform(key, (NY, FIELDS), jnp.float32, 0.995, 0.999)


def draw_backward_mult(key, part):
    key = jax.random.fold_in(key, 23)
    return jax.random.uniform(key, (NY, FIELDS), jnp.float32, 0.995, 0.999)


def block_levels(stream_key, shape, pieces, low, largest):
    loudness, own = 1.0, jax.random.fold_in(stream_key, 6)
    for position, shards_of in pieces:
        draws = jnp.exp(jax.random.uniform(jax.random.fold_in(own, position), (shards_of,), jnp.float32, low / len(pieces), largest / len(pieces)))
        loudness = loudness * jnp.repeat(draws, shape[position] // shards_of).reshape([-1 if axis == position else 1 for axis in range(len(shape))])
    return loudness


def noise(stream_key, extent, scale, bound, cuts=(), kind=jnp.bfloat16):
    array = scale * jax.random.normal(stream_key, extent, jnp.float32)
    if cuts:
        array = array * block_levels(stream_key, extent, cuts, -0.22, 0.18)
    return jnp.clip(array, -bound, bound).astype(kind)


def setup_inputs(seed: int = 0) -> dict:
    seeds = jax.random.split(jax.random.key(seed), 6)
    fields = noise(seeds[0], (NY, FIELDS, NZ, NX), 1.0, 6.0, ((0, 32), (2, 8)), jnp.float32)
    kappa = jnp.clip(0.02 + 0.14 * jax.random.uniform(seeds[1], (NY, NZ, NX), jnp.float32) ** block_levels(seeds[1], (NY, NZ, NX), ((0, 32), (1, 8)), -0.2, 0.2), 0.02, 0.16)
    forward_mult = draw_forward_mult(jax.random.fold_in(seeds[5], 71), 0)
    pivot_inv = jnp.clip(jnp.exp(math.log(0.001) - 2.3025852 * jax.random.uniform(seeds[3], (NY, FIELDS), jnp.float32) ** block_levels(seeds[3], (NY, FIELDS), ((0, 32),), -0.2, 0.2)), 0.0001, 0.001)
    backward_mult = draw_backward_mult(jax.random.fold_in(seeds[5], 71), 0)
    return dict(fields=fields, kappa=kappa, forward_mult=forward_mult, pivot_inv=pivot_inv, backward_mult=backward_mult)


def explicit_part(fields, kappa):
    padded = jnp.pad(fields, ((1, 1), (0, 0), (0, 0), (0, 0)))
    beside_all = padded[2:] + padded[:-2]
    beside_all = beside_all + jnp.roll(fields, 1, 2) + jnp.roll(fields, -1, 2)
    beside_all = beside_all + jnp.roll(fields, 1, 3) + jnp.roll(fields, -1, 3)
    right = fields + kappa[:, None] * (beside_all - 6.0 * fields)
    lifted = right[:, 2] + 0.5 * fields[:, 0]
    return jnp.concatenate([right[:, :2], lifted[:, None], right[:, 3:]], axis=1)


def reference(fields, kappa, forward_mult, pivot_inv, backward_mult):
    right = explicit_part(fields, kappa)

    def forward_step(carry, items):
        value, factor = items
        carry = value + factor[:, None, None] * carry
        return carry, carry

    start = jnp.zeros(right.shape[1:], jnp.float32)
    _, swept = lax.scan(forward_step, start, (right, forward_mult))

    def backward_step(carry, items):
        value, scale, factor = items
        carry = scale[:, None, None] * value + factor[:, None, None] * carry
        return carry, carry

    _, solved = lax.scan(backward_step, start, (swept, pivot_inv, backward_mult), reverse=True)
    return solved
```

```python
import jax
import jax.numpy as jnp
from jax import lax
from jax.experimental import pallas as pl
from jax.experimental.pallas import tpu as pltpu
from jax.sharding import Mesh
from jax.sharding import PartitionSpec as P

GY = ("y", "z")
GZ = ("x", "c")
FIELDS = 4
TILE = 8
STEP = 8
ROWS = 2 * FIELDS + 1
COEF_LANES = 8

VMEM = pl.BlockSpec(memory_space=pltpu.VMEM)
SMEM = pl.BlockSpec(memory_space=pltpu.SMEM)
HBM = pl.BlockSpec(memory_space=pltpu.HBM)
f32 = jnp.float32


def row_of(shape):
    return lax.broadcasted_iota(jnp.int32, shape, 0)


def lane_of(shape):
    return lax.broadcasted_iota(jnp.int32, shape, 1)


def collect(side, fields, inner, outer, near, far, sems):
    rows, _, span, _ = fields.shape
    z_near = jnp.where(side[0] == 0, span - 1, 0)
    j_near = jnp.where(side[1] == 0, rows - 1, 0)
    copies = [
        pltpu.make_async_copy(fields.at[:, :, pl.ds(span - 1 - z_near, 1)], outer, sems.at[0]),
        pltpu.make_async_copy(fields.at[:, :, pl.ds(z_near, 1)], inner, sems.at[1]),
        pltpu.make_async_copy(fields.at[j_near], near, sems.at[2]),
        pltpu.make_async_copy(fields.at[rows - 1 - j_near], far, sems.at[3]),
    ]
    for copy in copies:
        copy.start()
    for copy in copies:
        copy.wait()


def interior(fields, kappa, fwd, piv, bwd, base, last, first, rim, walls, held, weight, sweep, sems):
    rows, _, span, lanes = fields.shape
    tiles = span // TILE
    tile = (TILE, lanes)
    sub = row_of(tile)
    zero = jnp.zeros(tile, f32)
    chunks = rows // STEP

    def load(c):
        here = pl.ds(c * STEP, STEP)
        return (
            pltpu.make_async_copy(fields.at[here], held.at[pl.ds(1 + c * STEP, STEP)], sems.at[0, c]),
            pltpu.make_async_copy(kappa.at[here], weight.at[here], sems.at[1, c]),
        )

    for c in range(chunks):
        for copy in load(c):
            copy.start()
    for f in range(FIELDS):
        for v in range(tiles):
            held[0, f, pl.ds(v * TILE, TILE)] = zero
            held[rows + 1, f, pl.ds(v * TILE, TILE)] = zero
    for copy in load(0):
        copy.wait()

    def forward(c, carry):
        @pl.when(c < chunks - 1)
        def _():
            for copy in load(c + 1):
                copy.wait()

        state = list(carry)
        for i in range(STEP):
            j = c * STEP + i
            rim[j] = jnp.where(sub < FIELDS, weight[j, pl.ds(0, 1)], weight[j, pl.ds(span - 1, 1)])
        for f in range(FIELDS):
            for v in range(tiles):
                here = pl.ds(v * TILE, TILE)
                k = f * tiles + v
                under = held[c * STEP, f, here]
                x = held[c * STEP + 1, f, here]
                for i in range(STEP):
                    j = c * STEP + i
                    over = held[j + 2, f, here]
                    if v == 0:
                        left = jnp.where(sub == 0, 0.0, pltpu.roll(x, 1, 0))
                    else:
                        left = held[j + 1, f, pl.ds(v * TILE - 1, TILE)]
                    if v == tiles - 1:
                        right = jnp.where(sub == TILE - 1, 0.0, pltpu.roll(x, TILE - 1, 0))
                    else:
                        right = held[j + 1, f, pl.ds(v * TILE + 1, TILE)]
                    around = (left + right) + (pltpu.roll(x, 1, 1) + pltpu.roll(x, lanes - 1, 1))
                    around = around + (under + over)
                    new = x + weight[j, here] * (around - 6.0 * x)
                    if f == 2:
                        new = new + 0.5 * held[j + 1, 0, here]
                    state[k] = new + fwd[f, j] * state[k]
                    sweep[j, f, here] = state[k]
                    under, x = x, over
        return tuple(state)

    start = (zero,) * (FIELDS * tiles)
    state = lax.fori_loop(0, chunks, forward, start)
    for f in range(FIELDS):
        for v in range(tiles):
            last[f, pl.ds(v * TILE, TILE)] = state[f * tiles + v]

    def store(c):
        here = pl.ds(c * STEP, STEP)
        return pltpu.make_async_copy(sweep.at[here], base.at[here], sems.at[0, c])

    def backward(t, carry):
        state = list(carry)
        for i in range(STEP):
            j = rows - 1 - (t * STEP + i)
            for f in range(FIELDS):
                p, m = piv[f, j], bwd[f, j]
                for v in range(tiles):
                    k = f * tiles + v
                    here = pl.ds(v * TILE, TILE)
                    state[k] = p * sweep[j, f, here] + m * state[k]
                    sweep[j, f, here] = state[k]
        store(chunks - 1 - t).start()
        return tuple(state)

    state = lax.fori_loop(0, chunks, backward, start)
    for f in range(FIELDS):
        for v in range(tiles):
            first[f, pl.ds(v * TILE, TILE)] = state[f * tiles + v]
    walls[0] = weight[0]
    walls[1] = weight[rows - 1]
    for c in range(chunks):
        store(c).wait()


def edges(side, last, first, rim, walls, inner, outer, near, far, fwd, piv, bwd, fix, packed, entry, resp, ends):
    nf, span, lanes = last.shape
    rows = fix.shape[0]
    tiles = span // TILE
    tile = (TILE, lanes)
    sub = row_of(tile)
    low, high = sub == 0, sub == TILE - 1
    upper = sub < FIELDS
    flip = jnp.broadcast_to(side[0], tile) == 1
    even = jnp.broadcast_to(side[1], tile) == 0
    zero, one = jnp.zeros(tile, f32), jnp.ones(tile, f32)
    twice = lambda x: jnp.concatenate([x, x], axis=0)
    fwd8, piv8, bwd8 = twice(fwd[...]), twice(piv[...]), twice(bwd[...])
    column = lambda x, j: jnp.broadcast_to(x[:, j : j + 1], tile)

    state, q = zero, one
    prods = []
    for j in range(rows):
        x = jnp.where(upper == flip, twice(inner[j, :, 0]), twice(outer[j, :, 0]))
        m = column(fwd8, j)
        state = rim[j] * x + m * state
        fix[j] = state
        if j:
            q = q * m
        resp[j] = q
    top, a, r = zero, zero, one
    for j in reversed(range(rows)):
        p, m = column(piv8, j), column(bwd8, j)
        top = p * fix[j] + m * top
        fix[j] = top
        a = p * resp[j] + m * a
        if j < rows - 1:
            r = r * m
        resp[j] = jnp.where(upper, a, r)
    enters, leaves, lift = column(fwd8, 0), column(bwd8, rows - 1), column(piv8, rows - 1)
    ends[...] = jnp.where(upper, enters, leaves)

    for f in range(FIELDS):
        one_row = lambda x: x[f : f + 1]
        for v in range(tiles):
            here = pl.ds(v * TILE, TILE)
            below = jnp.where(even, far[f, here], near[f, here])
            above = jnp.where(even, near[f, here], far[f, here])
            under = walls[0, here] * below
            over = walls[1, here] * above
            lifted = one_row(lift) * over
            value = last[f, here] + one_row(q) * under + over
            answer = first[f, here] + one_row(a) * under + one_row(r) * lifted
            if v == 0:
                value = value + jnp.where(low, state[f : f + 1], 0.0)
                answer = answer + jnp.where(low, top[f : f + 1], 0.0)
            if v == tiles - 1:
                value = value + jnp.where(high, state[FIELDS + f : FIELDS + f + 1], 0.0)
                answer = answer + jnp.where(high, top[FIELDS + f : FIELDS + f + 1], 0.0)
            entry[0, f, here] = under
            entry[1, f, here] = lifted
            packed[pl.ds(v * TILE * ROWS + f, TILE, stride=ROWS)] = value
            packed[pl.ds(v * TILE * ROWS + FIELDS + f, TILE, stride=ROWS)] = answer
    group = lane_of(tile) // COEF_LANES
    out = zero
    for i, c in enumerate((q * enters, a * enters, r * leaves)):
        for f in range(FIELDS):
            out = jnp.where(group == i * FIELDS + f, c[f : f + 1], out)
    for v in range(tiles):
        packed[pl.ds(v * TILE * ROWS + 2 * FIELDS, TILE, stride=ROWS)] = out


def solve(got, out):
    count = got.shape[0] // ROWS
    tile = (TILE, got.shape[1])
    sub, lane = row_of(tile), lane_of(tile)
    upper = sub < FIELDS
    zero = jnp.zeros(tile, f32)

    def coefficient(k, i):
        here = lane == (i * FIELDS + sub % FIELDS) * COEF_LANES
        row = jnp.broadcast_to(got[pl.ds(k * ROWS + 2 * FIELDS, 1)], tile)
        return jnp.broadcast_to(jnp.sum(jnp.where(here, row, 0.0), axis=1, keepdims=True), tile)

    e, entering = zero, []
    for k in range(count):
        both = got[pl.ds(k * ROWS, TILE)]
        entering.append(e)
        out[k] = e
        e = jnp.where(upper, both, pltpu.roll(both, FIELDS, 0)) + coefficient(k, 0) * e
    b = zero
    for k in reversed(range(count)):
        both = got[pl.ds(k * ROWS, TILE)]
        e = out[k]
        out[k] = jnp.where(upper, e, b)
        b = jnp.where(upper, pltpu.roll(both, FIELDS, 0), both) + coefficient(k, 1) * e + coefficient(k, 2) * b


def finish(base, got, entry, resp, fix, ends, out, start, stage, sems):
    rows, _, span, lanes = out.shape
    tiles = span // TILE
    sub = row_of((TILE, lanes))
    chunks = rows // STEP

    def load(c):
        here = pl.ds(c * STEP, STEP)
        return pltpu.make_async_copy(base.at[here], stage.at[here], sems.at[0, c])

    def store(c):
        here = pl.ds(c * STEP, STEP)
        return pltpu.make_async_copy(stage.at[here], out.at[here], sems.at[1, c])

    for c in range(chunks):
        load(c).start()
    for f in range(FIELDS):
        for v in range(tiles):
            here = pl.ds(v * TILE, TILE)
            e = got[pl.ds(v * TILE * TILE + f, TILE, stride=TILE)]
            b = got[pl.ds(v * TILE * TILE + FIELDS + f, TILE, stride=TILE)]
            start[0, f, here] = ends[pl.ds(f, 1)] * e + entry[0, f, here]
            start[1, f, here] = ends[pl.ds(FIELDS + f, 1)] * b + entry[1, f, here]

    def body(c, carry):
        load(c).wait()
        for f in range(FIELDS):
            u = [start[0, f, pl.ds(v * TILE, TILE)] for v in range(tiles)]
            w = [start[1, f, pl.ds(v * TILE, TILE)] for v in range(tiles)]
            for i in range(STEP):
                j = c * STEP + i
                a, r = resp[j, pl.ds(f, 1)], resp[j, pl.ds(FIELDS + f, 1)]
                for v in range(tiles):
                    here = pl.ds(v * TILE, TILE)
                    x = stage[j, f, here] + a * u[v] + r * w[v]
                    if v == 0:
                        x = x + jnp.where(sub == 0, fix[j, pl.ds(f, 1)], 0.0)
                    if v == tiles - 1:
                        x = x + jnp.where(sub == TILE - 1, fix[j, pl.ds(FIELDS + f, 1)], 0.0)
                    stage[j, f, here] = x
        store(c).start()
        return carry

    lax.fori_loop(0, chunks, body, 0)
    for c in range(chunks):
        store(c).wait()


def params(mib):
    return pltpu.CompilerParams(vmem_limit_bytes=mib << 20)


def on_device(fields, kappa, fwd, piv, bwd):
    rows, nf, span, lanes = fields.shape
    shape = lambda *s: jax.ShapeDtypeStruct(s, f32)
    in_hbm = lambda x: pltpu.with_memory_space_constraint(x, pltpu.HBM)
    count = lax.axis_size(GY)
    around = lax.axis_size(GZ)
    pairs = lambda n, first: [(i, i + 1) for i in range(first, n - 1, 2)]
    both = lambda ends: ends + [(b, a) for a, b in ends]
    side = jnp.stack([lax.axis_index("c"), lax.rem(lax.axis_index("z"), 2)]).astype(jnp.int32)
    fwd, piv, bwd = fwd.T, piv.T, bwd.T
    fields, kappa = in_hbm(fields), in_hbm(kappa)
    inner, outer, near, far = pl.pallas_call(
        collect,
        out_shape=(shape(rows, nf, 1, lanes),) * 2 + (shape(nf, span, lanes),) * 2,
        in_specs=[SMEM, HBM],
        out_specs=(VMEM,) * 4,
        scratch_shapes=[pltpu.SemaphoreType.DMA((4,))],
        compiler_params=params(4),
        name="collect",
    )(side, fields)
    outer = lax.ppermute(outer, GZ, both(pairs(around, 1) + [(around - 1, 0)]))
    far = lax.ppermute(far, GY, both(pairs(count, 1)))
    near = lax.ppermute(near, GY, both(pairs(count, 0)))
    inner = lax.ppermute(inner, GZ, both(pairs(around, 0)))

    chunks = rows // STEP
    base, last, first, rim, walls = pl.pallas_call(
        interior,
        out_shape=(
            pltpu.HBM((rows, nf, span, lanes), f32),
            shape(nf, span, lanes),
            shape(nf, span, lanes),
            shape(rows, TILE, lanes),
            shape(2, span, lanes),
        ),
        in_specs=[HBM, HBM, SMEM, SMEM, SMEM],
        out_specs=(HBM,) + (VMEM,) * 4,
        scratch_shapes=[
            pltpu.VMEM((rows + 2, nf, span, lanes), f32),
            pltpu.VMEM((rows, span, lanes), f32),
            pltpu.VMEM((rows, nf, span, lanes), f32),
            pltpu.SemaphoreType.DMA((2, chunks)),
        ],
        compiler_params=params(24),
        cost_estimate=pl.CostEstimate(flops=20 * fields.size, bytes_accessed=9 * fields.size, transcendentals=0),
        name="interior",
    )(fields, kappa, fwd, piv, bwd)

    fix, packed, entry, resp, ends = pl.pallas_call(
        edges,
        out_shape=(
            shape(rows, TILE, lanes),
            shape(span * ROWS, lanes),
            shape(2, nf, span, lanes),
            shape(rows, TILE, lanes),
            shape(TILE, lanes),
        ),
        in_specs=[SMEM] + [VMEM] * 11,
        out_specs=(VMEM,) * 5,
        compiler_params=params(4),
        name="edges",
    )(side, last, first, rim, walls, inner, outer, near, far, fwd, piv, bwd)

    got = lax.all_to_all(packed.reshape(count, ROWS, 1, lanes), GY, 0, 0)
    out = pl.pallas_call(
        solve,
        out_shape=shape(count, TILE, lanes),
        in_specs=[VMEM],
        out_specs=VMEM,
        compiler_params=params(4),
        name="solve",
    )(got.reshape(count * ROWS, lanes))
    back = lax.all_to_all(out, GY, 0, 0)
    return pl.pallas_call(
        finish,
        out_shape=shape(rows, nf, span, lanes),
        in_specs=[HBM] + [VMEM] * 5,
        out_specs=HBM,
        scratch_shapes=[
            pltpu.VMEM((2, nf, span, lanes), f32),
            pltpu.VMEM((rows, nf, span, lanes), f32),
            pltpu.SemaphoreType.DMA((2, chunks)),
        ],
        compiler_params=params(16),
        name="finish",
    )(in_hbm(base), back.reshape(count * TILE, lanes), entry, resp, fix, ends)


def solution(mesh):
    nz = 8 if mesh.shape["gy"] % 8 == 0 else 1
    split = Mesh(mesh.devices.reshape(-1, nz, mesh.shape["gz"] // 2, 2), GY + GZ)
    placed = (P(GY, None, GZ, None), P(GY, GZ, None), P(GY, None), P(GY, None), P(GY, None))
    return jax.shard_map(
        on_device, mesh=split, in_specs=placed, out_specs=P(GY, None, GZ, None), check_vma=False
    )
```

```python
import jax
import jax.numpy as jnp
from jax import lax
from jax.experimental import pallas as pl
from jax.experimental.pallas import tpu as pltpu
from jax.sharding import Mesh
from jax.sharding import PartitionSpec as P

GY = ("y", "z")
GZ = ("x", "c")
FIELDS = 4
TILE = 8
STEP = 8
ROWS = 4 * FIELDS + 3

VMEM = pl.BlockSpec(memory_space=pltpu.VMEM)
SMEM = pl.BlockSpec(memory_space=pltpu.SMEM)
HBM = pl.BlockSpec(memory_space=pltpu.HBM)
f32 = jnp.float32


def row_of(shape):
    return lax.broadcasted_iota(jnp.int32, shape, 0)


def lane_of(shape):
    return lax.broadcasted_iota(jnp.int32, shape, 1)


def collect(side, fields, kappa, fwd, piv, bwd, weight, wide, inner, outer, sems):
    rows, _, span, lanes = fields.shape
    z_near = jnp.where(side[0] == 0, span - 1, 0)
    copies = [
        pltpu.make_async_copy(fields.at[:, :, pl.ds(span - 1 - z_near, 1)], outer, sems.at[0]),
        pltpu.make_async_copy(fields.at[:, :, pl.ds(z_near, 1)], inner, sems.at[1]),
        pltpu.make_async_copy(kappa, weight, sems.at[2]),
    ]
    for copy in copies:
        copy.start()
    for i, ref in enumerate((fwd, piv, bwd)):
        x = ref[...]
        x = jnp.concatenate([x, x], axis=0)
        for j in range(rows):
            wide[i, j] = jnp.broadcast_to(x[:, j : j + 1], (TILE, lanes))
    for copy in copies:
        copy.wait()


def forward(fields, weight, wide, sweep, state, layers, fresh):
    rows, _, span, lanes = sweep.shape
    tiles = span // TILE
    tile = (TILE, lanes)
    at = lambda v: pl.ds(v * TILE, TILE)
    sub = row_of(tile)
    total = rows // STEP
    layers[0] = fields[rows - 1]
    layers[1] = fields[0]

    def beside(j, f, v, x):
        if v == 0:
            low = jnp.where(sub == 0, 0.0, pltpu.roll(x, 1, 0))
        else:
            low = fields[j, f, pl.ds(v * TILE - 1, TILE)]
        if v == tiles - 1:
            return low + jnp.where(sub == TILE - 1, 0.0, pltpu.roll(x, TILE - 1, 0))
        return low + fields[j, f, pl.ds(v * TILE + 1, TILE)]

    def update(c):
        above_first = jnp.where(jnp.broadcast_to(c, tile) > 0, 1.0, 0.0)
        below_last = jnp.where(jnp.broadcast_to(c, tile) < total - 1, 1.0, 0.0)
        for v in range(tiles):
            under = [fields[jnp.maximum(c * STEP - 1, 0), f, at(v)] * above_first for f in range(FIELDS)]
            here = [fields[c * STEP, f, at(v)] for f in range(FIELDS)]
            for i in range(STEP):
                j = c * STEP + i
                k = weight[j, at(v)]
                own = 1.0 - 6.0 * k
                half = 0.5 * here[0]
                for f in range(FIELDS):
                    x = here[f]
                    if i < STEP - 1:
                        over = fields[j + 1, f, at(v)]
                    else:
                        over = fields[jnp.minimum(j + 1, rows - 1), f, at(v)] * below_last
                    around = beside(j, f, v, x)
                    around = around + (pltpu.roll(x, 1, 1) + pltpu.roll(x, lanes - 1, 1))
                    around = around + (under[f] + over)
                    new = own * x + k * around
                    if f == 2:
                        new = new + half
                    fresh[i, f, at(v)] = new
                    under[f], here[f] = x, over

    def advance(c, carry):
        carry = list(carry)
        for i in range(STEP):
            j = c * STEP + i
            for f in range(FIELDS):
                m = wide[0, j, pl.ds(f, 1)]
                for v in range(tiles):
                    k = f * tiles + v
                    carry[k] = fresh[i, f, at(v)] + m * carry[k]
                    sweep[j, f, at(v)] = carry[k]
        return tuple(carry)

    def both(c, carry):
        carry = advance(c - 1, carry)
        update(c)
        return carry

    update(0)
    carry = lax.fori_loop(1, total, both, (jnp.zeros(tile, f32),) * (FIELDS * tiles))
    carry = advance(total - 1, carry)
    for f in range(FIELDS):
        for v in range(tiles):
            state[f, at(v)] = carry[f * tiles + v]


def backward(wide, sweep, base, first):
    rows, _, span, lanes = base.shape
    tiles = span // TILE
    at = lambda v: pl.ds(v * TILE, TILE)

    def body(t, state):
        state = list(state)
        for i in range(2 * STEP):
            j = rows - 1 - (t * 2 * STEP + i)
            for f in range(FIELDS):
                p, m = wide[1, j, pl.ds(f, 1)], wide[2, j, pl.ds(f, 1)]
                for v in range(tiles):
                    k = f * tiles + v
                    state[k] = p * base[j, f, at(v)] + m * state[k]
                    base[j, f, at(v)] = state[k]
        return tuple(state)

    start = (jnp.zeros((TILE, lanes), f32),) * (FIELDS * tiles)
    state = lax.fori_loop(0, rows // (2 * STEP), body, start)
    for f in range(FIELDS):
        for v in range(tiles):
            first[f, at(v)] = state[f * tiles + v]


def edges(side, base_in, last, first, kappa, inner, outer, layers, wide, base, fix, packed, resp):
    del base_in, base
    nf, span, lanes = last.shape
    rows = fix.shape[0]
    tiles = span // TILE
    tile = (TILE, lanes)
    sub, lane = row_of(tile), lane_of(tile)
    low, high = sub == 0, sub == TILE - 1
    upper = sub < FIELDS
    flip = jnp.broadcast_to(side[0], tile) == 1
    zero, one = jnp.zeros(tile, f32), jnp.ones(tile, f32)
    twice = lambda x: jnp.concatenate([x, x], axis=0)

    state, q = zero, one
    for j in range(rows):
        x = jnp.where(upper == flip, twice(inner[j, :, 0]), twice(outer[j, :, 0]))
        k = jnp.where(upper, kappa[j, pl.ds(0, 1)], kappa[j, pl.ds(span - 1, 1)])
        m = wide[0, j]
        state = k * x + m * state
        fix[j] = state
        if j:
            q = q * m
        resp[j] = q
    top, a, r = zero, zero, one
    for j in reversed(range(rows)):
        p, m = wide[1, j], wide[2, j]
        top = p * fix[j] + m * top
        fix[j] = top
        a = p * resp[j] + m * a
        if j < rows - 1:
            r = r * m
        resp[j] = jnp.where(upper, a, r)

    for v in range(tiles):
        here = pl.ds(v * TILE, TILE)
        put = lambda i, x: packed.__setitem__(pl.ds(v * TILE * ROWS + i, TILE, stride=ROWS), x)
        for f in range(FIELDS):
            value, answer = last[f, here], first[f, here]
            if v == 0:
                value = value + jnp.where(low, state[f : f + 1], 0.0)
                answer = answer + jnp.where(low, top[f : f + 1], 0.0)
            if v == tiles - 1:
                value = value + jnp.where(high, state[FIELDS + f : FIELDS + f + 1], 0.0)
                answer = answer + jnp.where(high, top[FIELDS + f : FIELDS + f + 1], 0.0)
            put(f, value)
            put(FIELDS + f, answer)
            put(2 * FIELDS + f, layers[0, f, here])
            put(3 * FIELDS + f, layers[1, f, here])
        put(4 * FIELDS, kappa[0, here])
        put(4 * FIELDS + 1, kappa[rows - 1, here])
    enters, leaves, lift = wide[0, 0], wide[2, rows - 1], wide[1, rows - 1]
    coefs = (
        jnp.where(upper, q, r * lift),
        jnp.where(upper, one, a),
        q * enters,
        a * enters,
        r * leaves,
        jnp.where(upper, enters, leaves),
        jnp.where(upper, one, lift),
    )
    out = zero
    for i, c in enumerate(coefs):
        out = jnp.where(lane == i * TILE + sub, c, out)
    out = jnp.broadcast_to(jnp.sum(out, axis=0, keepdims=True), tile)
    for v in range(tiles):
        packed[pl.ds(v * TILE * ROWS + ROWS - 1, TILE, stride=ROWS)] = out


def solve(got, base_in, out, base, entry):
    del base_in, base
    count = got.shape[0] // ROWS
    tile = (TILE, got.shape[1])
    sub, lane = row_of(tile), lane_of(tile)
    upper = sub < FIELDS
    zero = jnp.zeros(tile, f32)
    swap = lambda x: pltpu.roll(x, FIELDS, 0)

    def coefficient(k, i):
        row = jnp.broadcast_to(got[pl.ds(k * ROWS + ROWS - 1, 1)], tile)
        row = jnp.where(lane == i * TILE + sub, row, 0.0)
        return jnp.broadcast_to(jnp.sum(row, axis=1, keepdims=True), tile)

    def layer(k):
        return got[pl.ds(k * ROWS + 2 * FIELDS, TILE)] if 0 <= k < count else zero

    e = zero
    for k in range(count):
        weight = jnp.where(upper, got[pl.ds(k * ROWS + 4 * FIELDS, 1)], got[pl.ds(k * ROWS + 4 * FIELDS + 1, 1)])
        brought = weight * jnp.where(upper, layer(k - 1), layer(k + 1))
        both = got[pl.ds(k * ROWS, TILE)] + coefficient(k, 0) * brought + coefficient(k, 1) * swap(brought)
        entry[0, k] = both
        entry[1, k] = coefficient(k, 6) * brought
        out[k] = e
        e = jnp.where(upper, both, swap(both)) + coefficient(k, 2) * e
    b = zero
    for k in reversed(range(count)):
        both, e = entry[0, k], out[k]
        out[k] = coefficient(k, 5) * jnp.where(upper, e, b) + entry[1, k]
        b = jnp.where(upper, swap(both), both) + coefficient(k, 3) * e + coefficient(k, 4) * b


def finish(base, got, resp, fix, out, start, stage, sems):
    rows, _, span, lanes = out.shape
    tiles = span // TILE
    sub = row_of((TILE, lanes))
    chunks = rows // STEP

    def store(c):
        here = pl.ds(c * STEP, STEP)
        return pltpu.make_async_copy(stage.at[here], out.at[here], sems.at[1, c])

    for f in range(FIELDS):
        for v in range(tiles):
            here = pl.ds(v * TILE, TILE)
            start[0, f, here] = got[pl.ds(v * TILE * TILE + f, TILE, stride=TILE)]
            start[1, f, here] = got[pl.ds(v * TILE * TILE + FIELDS + f, TILE, stride=TILE)]

    def body(c, carry):
        for f in range(FIELDS):
            u = [start[0, f, pl.ds(v * TILE, TILE)] for v in range(tiles)]
            w = [start[1, f, pl.ds(v * TILE, TILE)] for v in range(tiles)]
            for i in range(STEP):
                j = c * STEP + i
                a, r = resp[j, pl.ds(f, 1)], resp[j, pl.ds(FIELDS + f, 1)]
                for v in range(tiles):
                    here = pl.ds(v * TILE, TILE)
                    x = base[j, f, here] + a * u[v] + r * w[v]
                    if v == 0:
                        x = x + jnp.where(sub == 0, fix[j, pl.ds(f, 1)], 0.0)
                    if v == tiles - 1:
                        x = x + jnp.where(sub == TILE - 1, fix[j, pl.ds(FIELDS + f, 1)], 0.0)
                    stage[j, f, here] = x
        store(c).start()
        return carry

    lax.fori_loop(0, chunks, body, 0)
    for c in range(chunks):
        store(c).wait()


def params(mib):
    return pltpu.CompilerParams(vmem_limit_bytes=mib << 20)


def on_device(fields, kappa, fwd, piv, bwd):
    rows, nf, span, lanes = fields.shape
    shape = lambda *s: jax.ShapeDtypeStruct(s, f32)
    vmem = lambda *s: pltpu.VMEM(s, f32)
    in_vmem = lambda x: pltpu.with_memory_space_constraint(x, pltpu.VMEM)
    in_hbm = lambda x: pltpu.with_memory_space_constraint(x, pltpu.HBM)
    count = lax.axis_size(GY)
    around = lax.axis_size(GZ)
    pairs = lambda n, first: [(i, i + 1) for i in range(first, n - 1, 2)]
    both = lambda ends: ends + [(b, a) for a, b in ends]
    side = lax.axis_index("c").astype(jnp.int32).reshape(1)
    fwd, piv, bwd = fwd.T, piv.T, bwd.T
    fields, kappa = in_hbm(fields), in_hbm(kappa)
    chunks = rows // STEP
    weight, wide, inner, outer = pl.pallas_call(
        collect,
        out_shape=(
            vmem(rows, span, lanes),
            vmem(3, rows, TILE, lanes),
            vmem(rows, nf, 1, lanes),
            vmem(rows, nf, 1, lanes),
        ),
        in_specs=[SMEM, HBM, HBM, VMEM, VMEM, VMEM],
        out_specs=(VMEM,) * 4,
        scratch_shapes=[pltpu.SemaphoreType.DMA((3,))],
        compiler_params=params(4),
        name="collect",
    )(side, *map(in_hbm, (fields, kappa, fwd, piv, bwd)))
    outer = lax.ppermute(outer, GZ, both(pairs(around, 1) + [(around - 1, 0)]))
    inner = lax.ppermute(inner, GZ, both(pairs(around, 0)))
    block = in_vmem(fields), in_vmem(weight), in_vmem(wide)
    sweep, last, layers = pl.pallas_call(
        forward,
        out_shape=(vmem(rows, nf, span, lanes), vmem(nf, span, lanes), vmem(2, nf, span, lanes)),
        in_specs=[VMEM] * 3,
        out_specs=(VMEM,) * 3,
        scratch_shapes=[pltpu.VMEM((STEP, nf, span, lanes), f32)],
        compiler_params=params(4),
        cost_estimate=pl.CostEstimate(flops=20 * fields.size, bytes_accessed=4 * fields.size, transcendentals=0),
        name="forward",
    )(*block)
    base, first = pl.pallas_call(
        backward,
        out_shape=(vmem(rows, nf, span, lanes), vmem(nf, span, lanes)),
        in_specs=[VMEM, VMEM],
        out_specs=(VMEM, VMEM),
        input_output_aliases={1: 0},
        compiler_params=params(4),
        cost_estimate=pl.CostEstimate(flops=1, bytes_accessed=1, transcendentals=0),
        name="backward",
    )(in_vmem(wide), in_vmem(sweep))

    base, fix, packed, resp = pl.pallas_call(
        edges,
        out_shape=(
            vmem(rows, nf, span, lanes),
            shape(rows, TILE, lanes),
            shape(span * ROWS, lanes),
            shape(rows, TILE, lanes),
        ),
        in_specs=[SMEM] + [VMEM] * 8,
        out_specs=(VMEM,) * 4,
        input_output_aliases={1: 0},
        compiler_params=params(4),
        name="edges",
    )(side, in_vmem(base), last, first, in_vmem(weight), inner, outer, layers, in_vmem(wide))

    got = lax.all_to_all(packed.reshape(count, ROWS, 1, lanes), GY, 0, 0)
    out, base = pl.pallas_call(
        solve,
        out_shape=(shape(count, TILE, lanes), pltpu.VMEM((rows, nf, span, lanes), f32)),
        in_specs=[VMEM, VMEM],
        out_specs=(VMEM, VMEM),
        input_output_aliases={1: 1},
        scratch_shapes=[pltpu.VMEM((2, count, TILE, lanes), f32)],
        compiler_params=params(4),
        name="solve",
    )(got.reshape(count * ROWS, lanes), in_vmem(base))
    back = lax.all_to_all(out, GY, 0, 0)
    return pl.pallas_call(
        finish,
        out_shape=shape(rows, nf, span, lanes),
        in_specs=[VMEM] * 4,
        out_specs=HBM,
        scratch_shapes=[
            pltpu.VMEM((2, nf, span, lanes), f32),
            pltpu.VMEM((rows, nf, span, lanes), f32),
            pltpu.SemaphoreType.DMA((2, chunks)),
        ],
        compiler_params=params(16),
        name="finish",
    )(in_vmem(base), back.reshape(count * TILE, lanes), resp, fix)


def solution(mesh):
    nz = 8 if mesh.shape["gy"] % 8 == 0 else 1
    split = Mesh(mesh.devices.reshape(-1, nz, mesh.shape["gz"] // 2, 2), GY + GZ)
    placed = (P(GY, None, GZ, None), P(GY, GZ, None), P(GY, None), P(GY, None), P(GY, None))
    return jax.shard_map(
        on_device, mesh=split, in_specs=placed, out_specs=P(GY, None, GZ, None), check_vma=False
    )
```

```python
import jax
import jax.numpy as jnp
from jax import lax
from jax.experimental import pallas as pl
from jax.experimental.pallas import tpu as pltpu
from jax.sharding import Mesh
from jax.sharding import PartitionSpec as P

GY = ("y", "z")
GZ = ("x", "c")
FIELDS = 4
TILE = 8
STEP = 8
ROWS = 4 * FIELDS + 3

VMEM = pl.BlockSpec(memory_space=pltpu.VMEM)
SMEM = pl.BlockSpec(memory_space=pltpu.SMEM)
HBM = pl.BlockSpec(memory_space=pltpu.HBM)
f32 = jnp.float32


def row_of(shape):
    return lax.broadcasted_iota(jnp.int32, shape, 0)


def lane_of(shape):
    return lax.broadcasted_iota(jnp.int32, shape, 1)


def collect(side, fields, kappa, fwd, piv, bwd, weight, wide, inner, outer, narrow, sems):
    rows, _, span, lanes = fields.shape
    z_near = jnp.where(side[0] == 0, span - 1, 0)
    copies = [
        pltpu.make_async_copy(fields.at[:, :, pl.ds(span - 1 - z_near, 1)], outer, sems.at[0]),
        pltpu.make_async_copy(fields.at[:, :, pl.ds(z_near, 1)], inner, sems.at[1]),
        pltpu.make_async_copy(kappa, weight, sems.at[2]),
    ]
    small = [pltpu.make_async_copy(ref, narrow.at[i], sems.at[3 + i]) for i, ref in enumerate((fwd, piv, bwd))]
    for copy in small + copies:
        copy.start()
    for copy in small:
        copy.wait()
    for i in range(3):
        x = narrow[i]
        x = jnp.concatenate([x, x], axis=0)
        for j in range(rows):
            wide[i, j] = jnp.broadcast_to(x[:, j : j + 1], (TILE, lanes))
    for copy in copies:
        copy.wait()


def forward(fields, weight, wide, sweep, state, layers, fresh):
    rows, _, span, lanes = sweep.shape
    tiles = span // TILE
    tile = (TILE, lanes)
    at = lambda v: pl.ds(v * TILE, TILE)
    sub = row_of(tile)
    total = rows // STEP
    layers[0] = fields[rows - 1]
    layers[1] = fields[0]

    def beside(j, f, v, x):
        if v == 0:
            low = jnp.where(sub == 0, 0.0, pltpu.roll(x, 1, 0))
        else:
            low = fields[j, f, pl.ds(v * TILE - 1, TILE)]
        if v == tiles - 1:
            return low + jnp.where(sub == TILE - 1, 0.0, pltpu.roll(x, TILE - 1, 0))
        return low + fields[j, f, pl.ds(v * TILE + 1, TILE)]

    def update(c):
        above_first = jnp.where(jnp.broadcast_to(c, tile) > 0, 1.0, 0.0)
        below_last = jnp.where(jnp.broadcast_to(c, tile) < total - 1, 1.0, 0.0)
        for v in range(tiles):
            under = [fields[jnp.maximum(c * STEP - 1, 0), f, at(v)] * above_first for f in range(FIELDS)]
            here = [fields[c * STEP, f, at(v)] for f in range(FIELDS)]
            for i in range(STEP):
                j = c * STEP + i
                k = weight[j, at(v)]
                own = 1.0 - 6.0 * k
                half = 0.5 * here[0]
                for f in range(FIELDS):
                    x = here[f]
                    if i < STEP - 1:
                        over = fields[j + 1, f, at(v)]
                    else:
                        over = fields[jnp.minimum(j + 1, rows - 1), f, at(v)] * below_last
                    around = beside(j, f, v, x)
                    around = around + (pltpu.roll(x, 1, 1) + pltpu.roll(x, lanes - 1, 1))
                    around = around + (under[f] + over)
                    new = own * x + k * around
                    if f == 2:
                        new = new + half
                    fresh[i, f, at(v)] = new
                    under[f], here[f] = x, over

    def advance(c, carry):
        carry = list(carry)
        for i in range(STEP):
            j = c * STEP + i
            for f in range(FIELDS):
                m = wide[0, j, pl.ds(f, 1)]
                for v in range(tiles):
                    k = f * tiles + v
                    carry[k] = fresh[i, f, at(v)] + m * carry[k]
                    sweep[j, f, at(v)] = carry[k]
        return tuple(carry)

    def both(c, carry):
        carry = advance(c - 1, carry)
        update(c)
        return carry

    update(0)
    carry = lax.fori_loop(1, total, both, (jnp.zeros(tile, f32),) * (FIELDS * tiles))
    carry = advance(total - 1, carry)
    for f in range(FIELDS):
        for v in range(tiles):
            state[f, at(v)] = carry[f * tiles + v]


def backward(wide, sweep, base, first):
    rows, _, span, lanes = base.shape
    tiles = span // TILE
    at = lambda v: pl.ds(v * TILE, TILE)

    def body(t, state):
        state = list(state)
        for i in range(2 * STEP):
            j = rows - 1 - (t * 2 * STEP + i)
            for f in range(FIELDS):
                p, m = wide[1, j, pl.ds(f, 1)], wide[2, j, pl.ds(f, 1)]
                for v in range(tiles):
                    k = f * tiles + v
                    state[k] = p * base[j, f, at(v)] + m * state[k]
                    base[j, f, at(v)] = state[k]
        return tuple(state)

    start = (jnp.zeros((TILE, lanes), f32),) * (FIELDS * tiles)
    state = lax.fori_loop(0, rows // (2 * STEP), body, start)
    for f in range(FIELDS):
        for v in range(tiles):
            first[f, at(v)] = state[f * tiles + v]


def edges(side, base_in, last, first, kappa, inner, outer, layers, wide, base, fix, packed, resp):
    del base_in, base
    nf, span, lanes = last.shape
    rows = fix.shape[0]
    tiles = span // TILE
    tile = (TILE, lanes)
    sub, lane = row_of(tile), lane_of(tile)
    low, high = sub == 0, sub == TILE - 1
    upper = sub < FIELDS
    flip = jnp.broadcast_to(side[0], tile) == 1
    zero, one = jnp.zeros(tile, f32), jnp.ones(tile, f32)
    twice = lambda x: jnp.concatenate([x, x], axis=0)

    state, q = zero, one
    for j in range(rows):
        x = jnp.where(upper == flip, twice(inner[j, :, 0]), twice(outer[j, :, 0]))
        k = jnp.where(upper, kappa[j, pl.ds(0, 1)], kappa[j, pl.ds(span - 1, 1)])
        m = wide[0, j]
        state = k * x + m * state
        fix[j] = state
        if j:
            q = q * m
        resp[j] = q
    top, a, r = zero, zero, one
    for j in reversed(range(rows)):
        p, m = wide[1, j], wide[2, j]
        top = p * fix[j] + m * top
        fix[j] = top
        a = p * resp[j] + m * a
        if j < rows - 1:
            r = r * m
        resp[j] = jnp.where(upper, a, r)

    for v in range(tiles):
        here = pl.ds(v * TILE, TILE)
        put = lambda i, x: packed.__setitem__(pl.ds(v * TILE * ROWS + i, TILE, stride=ROWS), x)
        for f in range(FIELDS):
            value, answer = last[f, here], first[f, here]
            if v == 0:
                value = value + jnp.where(low, state[f : f + 1], 0.0)
                answer = answer + jnp.where(low, top[f : f + 1], 0.0)
            if v == tiles - 1:
                value = value + jnp.where(high, state[FIELDS + f : FIELDS + f + 1], 0.0)
                answer = answer + jnp.where(high, top[FIELDS + f : FIELDS + f + 1], 0.0)
            put(f, value)
            put(FIELDS + f, answer)
            put(2 * FIELDS + f, layers[0, f, here])
            put(3 * FIELDS + f, layers[1, f, here])
        put(4 * FIELDS, kappa[0, here])
        put(4 * FIELDS + 1, kappa[rows - 1, here])
    enters, leaves, lift = wide[0, 0], wide[2, rows - 1], wide[1, rows - 1]
    coefs = (
        jnp.where(upper, q, r * lift),
        jnp.where(upper, one, a),
        q * enters,
        a * enters,
        r * leaves,
        jnp.where(upper, enters, leaves),
        jnp.where(upper, one, lift),
    )
    out = zero
    for i, c in enumerate(coefs):
        out = jnp.where(lane == i * TILE + sub, c, out)
    out = jnp.broadcast_to(jnp.sum(out, axis=0, keepdims=True), tile)
    for v in range(tiles):
        packed[pl.ds(v * TILE * ROWS + ROWS - 1, TILE, stride=ROWS)] = out


def solve(got, base_in, out, base, entry):
    del base_in, base
    count = got.shape[0] // ROWS
    tile = (TILE, got.shape[1])
    sub, lane = row_of(tile), lane_of(tile)
    upper = sub < FIELDS
    zero = jnp.zeros(tile, f32)
    swap = lambda x: pltpu.roll(x, FIELDS, 0)

    def coefficient(k, i):
        row = jnp.broadcast_to(got[pl.ds(k * ROWS + ROWS - 1, 1)], tile)
        row = jnp.where(lane == i * TILE + sub, row, 0.0)
        return jnp.broadcast_to(jnp.sum(row, axis=1, keepdims=True), tile)

    def layer(k):
        return got[pl.ds(k * ROWS + 2 * FIELDS, TILE)] if 0 <= k < count else zero

    e = zero
    for k in range(count):
        weight = jnp.where(upper, got[pl.ds(k * ROWS + 4 * FIELDS, 1)], got[pl.ds(k * ROWS + 4 * FIELDS + 1, 1)])
        brought = weight * jnp.where(upper, layer(k - 1), layer(k + 1))
        both = got[pl.ds(k * ROWS, TILE)] + coefficient(k, 0) * brought + coefficient(k, 1) * swap(brought)
        entry[0, k] = both
        entry[1, k] = coefficient(k, 6) * brought
        out[k] = e
        e = jnp.where(upper, both, swap(both)) + coefficient(k, 2) * e
    b = zero
    for k in reversed(range(count)):
        both, e = entry[0, k], out[k]
        out[k] = coefficient(k, 5) * jnp.where(upper, e, b) + entry[1, k]
        b = jnp.where(upper, swap(both), both) + coefficient(k, 3) * e + coefficient(k, 4) * b


def finish(base, got, resp, fix, out, start, stage, sems):
    rows, _, span, lanes = out.shape
    tiles = span // TILE
    sub = row_of((TILE, lanes))
    chunks = rows // STEP

    def store(c):
        here = pl.ds(c * STEP, STEP)
        return pltpu.make_async_copy(stage.at[here], out.at[here], sems.at[1, c])

    for f in range(FIELDS):
        for v in range(tiles):
            here = pl.ds(v * TILE, TILE)
            start[0, f, here] = got[pl.ds(v * TILE * TILE + f, TILE, stride=TILE)]
            start[1, f, here] = got[pl.ds(v * TILE * TILE + FIELDS + f, TILE, stride=TILE)]

    def body(c, carry):
        for f in range(FIELDS):
            u = [start[0, f, pl.ds(v * TILE, TILE)] for v in range(tiles)]
            w = [start[1, f, pl.ds(v * TILE, TILE)] for v in range(tiles)]
            for i in range(STEP):
                j = c * STEP + i
                a, r = resp[j, pl.ds(f, 1)], resp[j, pl.ds(FIELDS + f, 1)]
                for v in range(tiles):
                    here = pl.ds(v * TILE, TILE)
                    x = base[j, f, here] + a * u[v] + r * w[v]
                    if v == 0:
                        x = x + jnp.where(sub == 0, fix[j, pl.ds(f, 1)], 0.0)
                    if v == tiles - 1:
                        x = x + jnp.where(sub == TILE - 1, fix[j, pl.ds(FIELDS + f, 1)], 0.0)
                    stage[j, f, here] = x
        store(c).start()
        return carry

    lax.fori_loop(0, chunks, body, 0)
    for c in range(chunks):
        store(c).wait()


def params(mib):
    return pltpu.CompilerParams(vmem_limit_bytes=mib << 20)


def on_device(fields, kappa, fwd, piv, bwd):
    rows, nf, span, lanes = fields.shape
    shape = lambda *s: jax.ShapeDtypeStruct(s, f32)
    vmem = lambda *s: pltpu.VMEM(s, f32)
    in_vmem = lambda x: pltpu.with_memory_space_constraint(x, pltpu.VMEM)
    in_hbm = lambda x: pltpu.with_memory_space_constraint(x, pltpu.HBM)
    count = lax.axis_size(GY)
    around = lax.axis_size(GZ)
    pairs = lambda n, first: [(i, i + 1) for i in range(first, n - 1, 2)]
    both = lambda ends: ends + [(b, a) for a, b in ends]
    side = lax.axis_index("c").astype(jnp.int32).reshape(1)
    fwd, piv, bwd = fwd.T, piv.T, bwd.T
    fields, kappa = in_hbm(fields), in_hbm(kappa)
    chunks = rows // STEP
    weight, wide, inner, outer = pl.pallas_call(
        collect,
        out_shape=(
            vmem(rows, span, lanes),
            vmem(3, rows, TILE, lanes),
            vmem(rows, nf, 1, lanes),
            vmem(rows, nf, 1, lanes),
        ),
        in_specs=[SMEM] + [HBM] * 5,
        out_specs=(VMEM,) * 4,
        scratch_shapes=[pltpu.VMEM((3, nf, rows), f32), pltpu.SemaphoreType.DMA((6,))],
        compiler_params=params(4),
        name="collect",
    )(side, *map(in_hbm, (fields, kappa, fwd, piv, bwd)))
    outer = lax.ppermute(outer, GZ, both(pairs(around, 1) + [(around - 1, 0)]))
    inner = lax.ppermute(inner, GZ, both(pairs(around, 0)))
    block = in_vmem(fields), in_vmem(weight), in_vmem(wide)
    sweep, last, layers = pl.pallas_call(
        forward,
        out_shape=(vmem(rows, nf, span, lanes), vmem(nf, span, lanes), vmem(2, nf, span, lanes)),
        in_specs=[VMEM] * 3,
        out_specs=(VMEM,) * 3,
        scratch_shapes=[pltpu.VMEM((STEP, nf, span, lanes), f32)],
        compiler_params=params(4),
        cost_estimate=pl.CostEstimate(flops=20 * fields.size, bytes_accessed=4 * fields.size, transcendentals=0),
        name="forward",
    )(*block)
    base, first = pl.pallas_call(
        backward,
        out_shape=(vmem(rows, nf, span, lanes), vmem(nf, span, lanes)),
        in_specs=[VMEM, VMEM],
        out_specs=(VMEM, VMEM),
        input_output_aliases={1: 0},
        compiler_params=params(4),
        cost_estimate=pl.CostEstimate(flops=1, bytes_accessed=1, transcendentals=0),
        name="backward",
    )(in_vmem(wide), in_vmem(sweep))

    base, fix, packed, resp = pl.pallas_call(
        edges,
        out_shape=(
            vmem(rows, nf, span, lanes),
            shape(rows, TILE, lanes),
            shape(span * ROWS, lanes),
            shape(rows, TILE, lanes),
        ),
        in_specs=[SMEM] + [VMEM] * 8,
        out_specs=(VMEM,) * 4,
        input_output_aliases={1: 0},
        compiler_params=params(4),
        name="edges",
    )(side, in_vmem(base), last, first, in_vmem(weight), inner, outer, layers, in_vmem(wide))

    got = lax.all_to_all(packed.reshape(count, ROWS, 1, lanes), GY, 0, 0)
    out, base = pl.pallas_call(
        solve,
        out_shape=(shape(count, TILE, lanes), pltpu.VMEM((rows, nf, span, lanes), f32)),
        in_specs=[VMEM, VMEM],
        out_specs=(VMEM, VMEM),
        input_output_aliases={1: 1},
        scratch_shapes=[pltpu.VMEM((2, count, TILE, lanes), f32)],
        compiler_params=params(4),
        name="solve",
    )(got.reshape(count * ROWS, lanes), in_vmem(base))
    back = lax.all_to_all(out, GY, 0, 0)
    return pl.pallas_call(
        finish,
        out_shape=shape(rows, nf, span, lanes),
        in_specs=[VMEM] * 4,
        out_specs=HBM,
        scratch_shapes=[
            pltpu.VMEM((2, nf, span, lanes), f32),
            pltpu.VMEM((rows, nf, span, lanes), f32),
            pltpu.SemaphoreType.DMA((2, chunks)),
        ],
        compiler_params=params(16),
        name="finish",
    )(in_vmem(base), back.reshape(count * TILE, lanes), resp, fix)


def solution(mesh):
    nz = 8 if mesh.shape["gy"] % 8 == 0 else 1
    split = Mesh(mesh.devices.reshape(-1, nz, mesh.shape["gz"] // 2, 2), GY + GZ)
    placed = (P(GY, None, GZ, None), P(GY, GZ, None), P(GY, None), P(GY, None), P(GY, None))
    return jax.shard_map(
        on_device, mesh=split, in_specs=placed, out_specs=P(GY, None, GZ, None), check_vma=False
    )
```

```python
import jax
import jax.numpy as jnp
from jax import lax
from jax.experimental import pallas as pl
from jax.experimental.pallas import tpu as pltpu
from jax.sharding import Mesh
from jax.sharding import PartitionSpec as P

GY = ("y", "z")
GZ = ("x", "c")
FIELDS = 4
TILE = 8
STEP = 8
ROWS = 3 * FIELDS + 2

VMEM = pl.BlockSpec(memory_space=pltpu.VMEM)
SMEM = pl.BlockSpec(memory_space=pltpu.SMEM)
HBM = pl.BlockSpec(memory_space=pltpu.HBM)
f32 = jnp.float32


def row_of(shape):
    return lax.broadcasted_iota(jnp.int32, shape, 0)


def lane_of(shape):
    return lax.broadcasted_iota(jnp.int32, shape, 1)


def collect(side, odd, fields, kappa, fwd, piv, bwd, weight, wide, inner, outer, near, narrow, sems):
    rows, _, span, lanes = fields.shape
    z_near = jnp.where(side[0] == 0, span - 1, 0)
    copies = [
        pltpu.make_async_copy(fields.at[:, :, pl.ds(span - 1 - z_near, 1)], outer, sems.at[0]),
        pltpu.make_async_copy(fields.at[:, :, pl.ds(z_near, 1)], inner, sems.at[1]),
        pltpu.make_async_copy(fields.at[jnp.where(odd[0] == 0, rows - 1, 0)], near, sems.at[2]),
        pltpu.make_async_copy(kappa, weight, sems.at[3]),
    ]
    small = [pltpu.make_async_copy(ref, narrow.at[i], sems.at[4 + i]) for i, ref in enumerate((fwd, piv, bwd))]
    for copy in small + copies:
        copy.start()
    for copy in small:
        copy.wait()
    for i in range(3):
        x = narrow[i]
        x = jnp.concatenate([x, x], axis=0)
        for j in range(rows):
            wide[i, j] = jnp.broadcast_to(x[:, j : j + 1], (TILE, lanes))
    for copy in copies:
        copy.wait()


def forward(fields, weight, wide, sweep, state, layers, fresh):
    rows, _, span, lanes = sweep.shape
    tiles = span // TILE
    tile = (TILE, lanes)
    at = lambda v: pl.ds(v * TILE, TILE)
    sub = row_of(tile)
    total = rows // STEP
    layers[0] = fields[rows - 1]
    layers[1] = fields[0]

    def beside(j, f, v, x):
        if v == 0:
            low = jnp.where(sub == 0, 0.0, pltpu.roll(x, 1, 0))
        else:
            low = fields[j, f, pl.ds(v * TILE - 1, TILE)]
        if v == tiles - 1:
            return low + jnp.where(sub == TILE - 1, 0.0, pltpu.roll(x, TILE - 1, 0))
        return low + fields[j, f, pl.ds(v * TILE + 1, TILE)]

    def update(c):
        above_first = jnp.where(jnp.broadcast_to(c, tile) > 0, 1.0, 0.0)
        below_last = jnp.where(jnp.broadcast_to(c, tile) < total - 1, 1.0, 0.0)
        for v in range(tiles):
            under = [fields[jnp.maximum(c * STEP - 1, 0), f, at(v)] * above_first for f in range(FIELDS)]
            here = [fields[c * STEP, f, at(v)] for f in range(FIELDS)]
            for i in range(STEP):
                j = c * STEP + i
                k = weight[j, at(v)]
                own = 1.0 - 6.0 * k
                half = 0.5 * here[0]
                for f in range(FIELDS):
                    x = here[f]
                    if i < STEP - 1:
                        over = fields[j + 1, f, at(v)]
                    else:
                        over = fields[jnp.minimum(j + 1, rows - 1), f, at(v)] * below_last
                    around = beside(j, f, v, x)
                    around = around + (pltpu.roll(x, 1, 1) + pltpu.roll(x, lanes - 1, 1))
                    around = around + (under[f] + over)
                    new = own * x + k * around
                    if f == 2:
                        new = new + half
                    fresh[i, f, at(v)] = new
                    under[f], here[f] = x, over

    def advance(c, carry):
        carry = list(carry)
        for i in range(STEP):
            j = c * STEP + i
            for f in range(FIELDS):
                m = wide[0, j, pl.ds(f, 1)]
                for v in range(tiles):
                    k = f * tiles + v
                    carry[k] = fresh[i, f, at(v)] + m * carry[k]
                    sweep[j, f, at(v)] = carry[k]
        return tuple(carry)

    def both(c, carry):
        carry = advance(c - 1, carry)
        update(c)
        return carry

    update(0)
    carry = lax.fori_loop(1, total, both, (jnp.zeros(tile, f32),) * (FIELDS * tiles))
    carry = advance(total - 1, carry)
    for f in range(FIELDS):
        for v in range(tiles):
            state[f, at(v)] = carry[f * tiles + v]


def backward(wide, sweep, base, first):
    rows, _, span, lanes = base.shape
    tiles = span // TILE
    at = lambda v: pl.ds(v * TILE, TILE)

    def body(t, state):
        state = list(state)
        for i in range(2 * STEP):
            j = rows - 1 - (t * 2 * STEP + i)
            for f in range(FIELDS):
                p, m = wide[1, j, pl.ds(f, 1)], wide[2, j, pl.ds(f, 1)]
                for v in range(tiles):
                    k = f * tiles + v
                    state[k] = p * base[j, f, at(v)] + m * state[k]
                    base[j, f, at(v)] = state[k]
        return tuple(state)

    start = (jnp.zeros((TILE, lanes), f32),) * (FIELDS * tiles)
    state = lax.fori_loop(0, rows // (2 * STEP), body, start)
    for f in range(FIELDS):
        for v in range(tiles):
            first[f, at(v)] = state[f * tiles + v]


def edges(side, odd, base_in, last, first, kappa, inner, outer, near, layers, wide, base, fix, packed, resp, entry):
    del base_in, base
    nf, span, lanes = last.shape
    rows = fix.shape[0]
    tiles = span // TILE
    tile = (TILE, lanes)
    sub, lane = row_of(tile), lane_of(tile)
    low, high = sub == 0, sub == TILE - 1
    upper = sub < FIELDS
    flip = jnp.broadcast_to(side[0], tile) == 1
    even = jnp.broadcast_to(odd[0], tile) == 0
    zero, one = jnp.zeros(tile, f32), jnp.ones(tile, f32)
    twice = lambda x: jnp.concatenate([x, x], axis=0)

    state, q = zero, one
    for j in range(rows):
        x = jnp.where(upper == flip, twice(inner[j, :, 0]), twice(outer[j, :, 0]))
        k = jnp.where(upper, kappa[j, pl.ds(0, 1)], kappa[j, pl.ds(span - 1, 1)])
        m = wide[0, j]
        state = k * x + m * state
        fix[j] = state
        if j:
            q = q * m
        resp[j] = q
    top, a, r = zero, zero, one
    for j in reversed(range(rows)):
        p, m = wide[1, j], wide[2, j]
        top = p * fix[j] + m * top
        fix[j] = top
        a = p * resp[j] + m * a
        if j < rows - 1:
            r = r * m
        resp[j] = jnp.where(upper, a, r)

    lift = wide[1, rows - 1]
    by_value, by_answer = jnp.where(even, one, q), jnp.where(even, r * lift, a)
    for v in range(tiles):
        here = pl.ds(v * TILE, TILE)
        put = lambda i, x: packed.__setitem__(pl.ds(v * TILE * ROWS + i, TILE, stride=ROWS), x)
        bottom, roof = kappa[0, here], kappa[rows - 1, here]
        for f in range(FIELDS):
            brought = jnp.where(even, roof, bottom) * near[f, here]
            entry[0, f, here] = jnp.where(even, 0.0, brought)
            entry[1, f, here] = jnp.where(even, lift[f : f + 1] * brought, 0.0)
            value = last[f, here] + by_value[f : f + 1] * brought
            answer = first[f, here] + by_answer[f : f + 1] * brought
            if v == 0:
                value = value + jnp.where(low, state[f : f + 1], 0.0)
                answer = answer + jnp.where(low, top[f : f + 1], 0.0)
            if v == tiles - 1:
                value = value + jnp.where(high, state[FIELDS + f : FIELDS + f + 1], 0.0)
                answer = answer + jnp.where(high, top[FIELDS + f : FIELDS + f + 1], 0.0)
            put(f, value)
            put(FIELDS + f, answer)
            put(2 * FIELDS + f, jnp.where(even, layers[1, f, here], layers[0, f, here]))
        put(3 * FIELDS, jnp.where(even, bottom, roof))
    enters, leaves = wide[0, 0], wide[2, rows - 1]
    coefs = (
        jnp.where(upper, q, r * lift),
        jnp.where(upper, one, a),
        q * enters,
        a * enters,
        r * leaves,
        jnp.where(upper, enters, leaves),
        jnp.where(upper, one, lift),
    )
    out = zero
    for i, c in enumerate(coefs):
        out = jnp.where(lane == i * TILE + sub, c, out)
    out = jnp.broadcast_to(jnp.sum(out, axis=0, keepdims=True), tile)
    for v in range(tiles):
        packed[pl.ds(v * TILE * ROWS + ROWS - 1, TILE, stride=ROWS)] = out


def solve(got, base_in, out, base, entry):
    del base_in, base
    count = got.shape[0] // ROWS
    tile = (TILE, got.shape[1])
    sub, lane = row_of(tile), lane_of(tile)
    upper = sub < FIELDS
    zero = jnp.zeros(tile, f32)
    swap = lambda x: pltpu.roll(x, FIELDS, 0)

    def coefficient(k, i):
        row = jnp.broadcast_to(got[pl.ds(k * ROWS + ROWS - 1, 1)], tile)
        row = jnp.where(lane == i * TILE + sub, row, 0.0)
        return jnp.broadcast_to(jnp.sum(row, axis=1, keepdims=True), tile)

    twice = lambda x: jnp.concatenate([x, x], axis=0)
    e = zero
    for k in range(count):
        other = k + 1 if k % 2 else k - 1
        brought = zero
        if 0 <= other < count:
            layer = twice(got[pl.ds(other * ROWS + 2 * FIELDS, FIELDS)])
            brought = jnp.where(upper == (k % 2 == 0), got[pl.ds(k * ROWS + 3 * FIELDS, 1)] * layer, 0.0)
        both = got[pl.ds(k * ROWS, TILE)] + coefficient(k, 0) * brought + coefficient(k, 1) * swap(brought)
        entry[0, k] = both
        entry[1, k] = coefficient(k, 6) * brought
        out[k] = e
        e = jnp.where(upper, both, swap(both)) + coefficient(k, 2) * e
    b = zero
    for k in reversed(range(count)):
        both, e = entry[0, k], out[k]
        out[k] = coefficient(k, 5) * jnp.where(upper, e, b) + entry[1, k]
        b = jnp.where(upper, swap(both), both) + coefficient(k, 3) * e + coefficient(k, 4) * b


def finish(base, got, entry, resp, fix, out, start, stage, sems):
    rows, _, span, lanes = out.shape
    tiles = span // TILE
    sub = row_of((TILE, lanes))
    chunks = rows // STEP

    def store(c):
        here = pl.ds(c * STEP, STEP)
        return pltpu.make_async_copy(stage.at[here], out.at[here], sems.at[1, c])

    for f in range(FIELDS):
        for v in range(tiles):
            here = pl.ds(v * TILE, TILE)
            start[0, f, here] = got[pl.ds(v * TILE * TILE + f, TILE, stride=TILE)] + entry[0, f, here]
            start[1, f, here] = got[pl.ds(v * TILE * TILE + FIELDS + f, TILE, stride=TILE)] + entry[1, f, here]

    def body(c, carry):
        for f in range(FIELDS):
            u = [start[0, f, pl.ds(v * TILE, TILE)] for v in range(tiles)]
            w = [start[1, f, pl.ds(v * TILE, TILE)] for v in range(tiles)]
            for i in range(STEP):
                j = c * STEP + i
                a, r = resp[j, pl.ds(f, 1)], resp[j, pl.ds(FIELDS + f, 1)]
                for v in range(tiles):
                    here = pl.ds(v * TILE, TILE)
                    x = base[j, f, here] + a * u[v] + r * w[v]
                    if v == 0:
                        x = x + jnp.where(sub == 0, fix[j, pl.ds(f, 1)], 0.0)
                    if v == tiles - 1:
                        x = x + jnp.where(sub == TILE - 1, fix[j, pl.ds(FIELDS + f, 1)], 0.0)
                    stage[j, f, here] = x
        store(c).start()
        return carry

    lax.fori_loop(0, chunks, body, 0)
    for c in range(chunks):
        store(c).wait()


def params(mib):
    return pltpu.CompilerParams(vmem_limit_bytes=mib << 20)


def on_device(fields, kappa, fwd, piv, bwd):
    rows, nf, span, lanes = fields.shape
    shape = lambda *s: jax.ShapeDtypeStruct(s, f32)
    vmem = lambda *s: pltpu.VMEM(s, f32)
    in_vmem = lambda x: pltpu.with_memory_space_constraint(x, pltpu.VMEM)
    in_hbm = lambda x: pltpu.with_memory_space_constraint(x, pltpu.HBM)
    count = lax.axis_size(GY)
    around = lax.axis_size(GZ)
    pairs = lambda n, first: [(i, i + 1) for i in range(first, n - 1, 2)]
    both = lambda ends: ends + [(b, a) for a, b in ends]
    side = lax.axis_index("c").astype(jnp.int32).reshape(1)
    odd = (lax.axis_index("z") & 1).astype(jnp.int32).reshape(1)
    fwd, piv, bwd = fwd.T, piv.T, bwd.T
    fields, kappa = in_hbm(fields), in_hbm(kappa)
    chunks = rows // STEP
    weight, wide, inner, outer, near = pl.pallas_call(
        collect,
        out_shape=(
            vmem(rows, span, lanes),
            vmem(3, rows, TILE, lanes),
            vmem(rows, nf, 1, lanes),
            vmem(rows, nf, 1, lanes),
            vmem(nf, span, lanes),
        ),
        in_specs=[SMEM, SMEM] + [HBM] * 5,
        out_specs=(VMEM,) * 5,
        scratch_shapes=[pltpu.VMEM((3, nf, rows), f32), pltpu.SemaphoreType.DMA((7,))],
        compiler_params=params(4),
        name="collect",
    )(side, odd, *map(in_hbm, (fields, kappa, fwd, piv, bwd)))
    outer = lax.ppermute(outer, GZ, both(pairs(around, 1) + [(around - 1, 0)]))
    near = lax.ppermute(near, GY, both(pairs(count, 0)))
    inner = lax.ppermute(inner, GZ, both(pairs(around, 0)))
    block = in_vmem(fields), in_vmem(weight), in_vmem(wide)
    sweep, last, layers = pl.pallas_call(
        forward,
        out_shape=(vmem(rows, nf, span, lanes), vmem(nf, span, lanes), vmem(2, nf, span, lanes)),
        in_specs=[VMEM] * 3,
        out_specs=(VMEM,) * 3,
        scratch_shapes=[pltpu.VMEM((STEP, nf, span, lanes), f32)],
        compiler_params=params(4),
        cost_estimate=pl.CostEstimate(flops=20 * fields.size, bytes_accessed=4 * fields.size, transcendentals=0),
        name="forward",
    )(*block)
    base, first = pl.pallas_call(
        backward,
        out_shape=(vmem(rows, nf, span, lanes), vmem(nf, span, lanes)),
        in_specs=[VMEM, VMEM],
        out_specs=(VMEM, VMEM),
        input_output_aliases={1: 0},
        compiler_params=params(4),
        cost_estimate=pl.CostEstimate(flops=1, bytes_accessed=1, transcendentals=0),
        name="backward",
    )(in_vmem(wide), in_vmem(sweep))

    base, fix, packed, resp, entry = pl.pallas_call(
        edges,
        out_shape=(
            vmem(rows, nf, span, lanes),
            shape(rows, TILE, lanes),
            shape(span * ROWS, lanes),
            shape(rows, TILE, lanes),
            shape(2, nf, span, lanes),
        ),
        in_specs=[SMEM, SMEM] + [VMEM] * 9,
        out_specs=(VMEM,) * 5,
        input_output_aliases={2: 0},
        compiler_params=params(4),
        name="edges",
    )(side, odd, in_vmem(base), last, first, in_vmem(weight), inner, outer, near, layers, in_vmem(wide))

    got = lax.all_to_all(packed.reshape(count, ROWS, 1, lanes), GY, 0, 0)
    out, base = pl.pallas_call(
        solve,
        out_shape=(shape(count, TILE, lanes), pltpu.VMEM((rows, nf, span, lanes), f32)),
        in_specs=[VMEM, VMEM],
        out_specs=(VMEM, VMEM),
        input_output_aliases={1: 1},
        scratch_shapes=[pltpu.VMEM((2, count, TILE, lanes), f32)],
        compiler_params=params(4),
        name="solve",
    )(got.reshape(count * ROWS, lanes), in_vmem(base))
    back = lax.all_to_all(out, GY, 0, 0)
    return pl.pallas_call(
        finish,
        out_shape=shape(rows, nf, span, lanes),
        in_specs=[VMEM] * 5,
        out_specs=HBM,
        scratch_shapes=[
            pltpu.VMEM((2, nf, span, lanes), f32),
            pltpu.VMEM((rows, nf, span, lanes), f32),
            pltpu.SemaphoreType.DMA((2, chunks)),
        ],
        compiler_params=params(16),
        name="finish",
    )(in_vmem(base), back.reshape(count * TILE, lanes), entry, resp, fix)


def solution(mesh):
    nz = 8 if mesh.shape["gy"] % 8 == 0 else 1
    split = Mesh(mesh.devices.reshape(-1, nz, mesh.shape["gz"] // 2, 2), GY + GZ)
    placed = (P(GY, None, GZ, None), P(GY, GZ, None), P(GY, None), P(GY, None), P(GY, None))
    return jax.shard_map(
        on_device, mesh=split, in_specs=placed, out_specs=P(GY, None, GZ, None), check_vma=False
    )
```

```python
import jax
import jax.numpy as jnp
from jax import lax
from jax.experimental import pallas as pl
from jax.experimental.pallas import tpu as pltpu
from jax.sharding import Mesh
from jax.sharding import PartitionSpec as P

GY = ("y", "z")
GZ = ("x", "c")
FIELDS = 4
TILE = 8
LONG = 16
STEP = 8
ROWS = 3 * FIELDS + 2

VMEM = pl.BlockSpec(memory_space=pltpu.VMEM)
SMEM = pl.BlockSpec(memory_space=pltpu.SMEM)
HBM = pl.BlockSpec(memory_space=pltpu.HBM)
f32 = jnp.float32


def row_of(shape):
    return lax.broadcasted_iota(jnp.int32, shape, 0)


def lane_of(shape):
    return lax.broadcasted_iota(jnp.int32, shape, 1)


def collect(side, odd, fields, kappa, fwd, piv, bwd, weight, wide, inner, outer, near, narrow, sems):
    rows, _, span, lanes = fields.shape
    z_near = jnp.where(side[0] == 0, span - 1, 0)
    copies = [
        pltpu.make_async_copy(fields.at[:, :, pl.ds(span - 1 - z_near, 1)], outer, sems.at[0]),
        pltpu.make_async_copy(fields.at[:, :, pl.ds(z_near, 1)], inner, sems.at[1]),
        pltpu.make_async_copy(fields.at[jnp.where(odd[0] == 0, rows - 1, 0)], near, sems.at[2]),
        pltpu.make_async_copy(kappa, weight, sems.at[3]),
    ]
    small = [pltpu.make_async_copy(ref, narrow.at[i], sems.at[4 + i]) for i, ref in enumerate((fwd, piv, bwd))]
    for copy in small + copies:
        copy.start()
    for copy in small:
        copy.wait()
    for i in range(3):
        x = narrow[i]
        x = jnp.concatenate([x, x], axis=0)
        for j in range(rows):
            wide[i, j] = jnp.broadcast_to(x[:, j : j + 1], (TILE, lanes))
    for copy in copies:
        copy.wait()


def forward(fields, weight, wide, sweep, state, layers, fresh):
    rows, _, span, lanes = sweep.shape
    tiles = span // TILE
    tile = (TILE, lanes)
    at = lambda v: pl.ds(v * TILE, TILE)
    sub = row_of(tile)
    total = rows // LONG
    layers[0] = fields[rows - 1]
    layers[1] = fields[0]

    def beside(j, f, v, x):
        if v == 0:
            low = jnp.where(sub == 0, 0.0, pltpu.roll(x, 1, 0))
        else:
            low = fields[j, f, pl.ds(v * TILE - 1, TILE)]
        if v == tiles - 1:
            return low + jnp.where(sub == TILE - 1, 0.0, pltpu.roll(x, TILE - 1, 0))
        return low + fields[j, f, pl.ds(v * TILE + 1, TILE)]

    def update(c):
        above_first = jnp.where(jnp.broadcast_to(c, tile) > 0, 1.0, 0.0)
        below_last = jnp.where(jnp.broadcast_to(c, tile) < total - 1, 1.0, 0.0)
        for v in range(tiles):
            under = [fields[jnp.maximum(c * LONG - 1, 0), f, at(v)] * above_first for f in range(FIELDS)]
            here = [fields[c * LONG, f, at(v)] for f in range(FIELDS)]
            for i in range(LONG):
                j = c * LONG + i
                k = weight[j, at(v)]
                own = 1.0 - 6.0 * k
                half = 0.5 * here[0]
                for f in range(FIELDS):
                    x = here[f]
                    if i < LONG - 1:
                        over = fields[j + 1, f, at(v)]
                    else:
                        over = fields[jnp.minimum(j + 1, rows - 1), f, at(v)] * below_last
                    around = beside(j, f, v, x)
                    around = around + (pltpu.roll(x, 1, 1) + pltpu.roll(x, lanes - 1, 1))
                    around = around + (under[f] + over)
                    new = own * x + k * around
                    if f == 2:
                        new = new + half
                    fresh[i, f, at(v)] = new
                    under[f], here[f] = x, over

    def advance(c, carry):
        carry = list(carry)
        for i in range(LONG):
            j = c * LONG + i
            for f in range(FIELDS):
                m = wide[0, j, pl.ds(f, 1)]
                for v in range(tiles):
                    k = f * tiles + v
                    carry[k] = fresh[i, f, at(v)] + m * carry[k]
                    sweep[j, f, at(v)] = carry[k]
        return tuple(carry)

    def both(c, carry):
        carry = advance(c - 1, carry)
        update(c)
        return carry

    update(0)
    carry = lax.fori_loop(1, total, both, (jnp.zeros(tile, f32),) * (FIELDS * tiles))
    carry = advance(total - 1, carry)
    for f in range(FIELDS):
        for v in range(tiles):
            state[f, at(v)] = carry[f * tiles + v]


def backward(wide, sweep, base, first):
    rows, _, span, lanes = base.shape
    tiles = span // TILE
    at = lambda v: pl.ds(v * TILE, TILE)

    def body(t, state):
        state = list(state)
        for i in range(2 * STEP):
            j = rows - 1 - (t * 2 * STEP + i)
            for f in range(FIELDS):
                p, m = wide[1, j, pl.ds(f, 1)], wide[2, j, pl.ds(f, 1)]
                for v in range(tiles):
                    k = f * tiles + v
                    state[k] = p * base[j, f, at(v)] + m * state[k]
                    base[j, f, at(v)] = state[k]
        return tuple(state)

    start = (jnp.zeros((TILE, lanes), f32),) * (FIELDS * tiles)
    state = lax.fori_loop(0, rows // (2 * STEP), body, start)
    for f in range(FIELDS):
        for v in range(tiles):
            first[f, at(v)] = state[f * tiles + v]


def sweeps(fields, weight, wide, base, last, layers, first, fresh):
    forward(fields, weight, wide, base, last, layers, fresh)
    backward(wide, None, base, first)


def edges(side, odd, base_in, last, first, kappa, inner, outer, near, layers, wide, base, fix, packed, resp, entry):
    del base_in, base
    nf, span, lanes = last.shape
    rows = fix.shape[0]
    tiles = span // TILE
    tile = (TILE, lanes)
    sub, lane = row_of(tile), lane_of(tile)
    low, high = sub == 0, sub == TILE - 1
    upper = sub < FIELDS
    flip = jnp.broadcast_to(side[0], tile) == 1
    even = jnp.broadcast_to(odd[0], tile) == 0
    zero, one = jnp.zeros(tile, f32), jnp.ones(tile, f32)
    twice = lambda x: jnp.concatenate([x, x], axis=0)

    state, q = zero, one
    for j in range(rows):
        x = jnp.where(upper == flip, twice(inner[j, :, 0]), twice(outer[j, :, 0]))
        k = jnp.where(upper, kappa[j, pl.ds(0, 1)], kappa[j, pl.ds(span - 1, 1)])
        m = wide[0, j]
        state = k * x + m * state
        fix[j] = state
        if j:
            q = q * m
        resp[j] = q
    top, a, r = zero, zero, one
    for j in reversed(range(rows)):
        p, m = wide[1, j], wide[2, j]
        top = p * fix[j] + m * top
        fix[j] = top
        a = p * resp[j] + m * a
        if j < rows - 1:
            r = r * m
        resp[j] = jnp.where(upper, a, r)

    lift = wide[1, rows - 1]
    by_value, by_answer = jnp.where(even, one, q), jnp.where(even, r * lift, a)
    for v in range(tiles):
        here = pl.ds(v * TILE, TILE)
        put = lambda i, x: packed.__setitem__(pl.ds(v * TILE * ROWS + i, TILE, stride=ROWS), x)
        bottom, roof = kappa[0, here], kappa[rows - 1, here]
        for f in range(FIELDS):
            brought = jnp.where(even, roof, bottom) * near[f, here]
            entry[0, f, here] = jnp.where(even, 0.0, brought)
            entry[1, f, here] = jnp.where(even, lift[f : f + 1] * brought, 0.0)
            value = last[f, here] + by_value[f : f + 1] * brought
            answer = first[f, here] + by_answer[f : f + 1] * brought
            if v == 0:
                value = value + jnp.where(low, state[f : f + 1], 0.0)
                answer = answer + jnp.where(low, top[f : f + 1], 0.0)
            if v == tiles - 1:
                value = value + jnp.where(high, state[FIELDS + f : FIELDS + f + 1], 0.0)
                answer = answer + jnp.where(high, top[FIELDS + f : FIELDS + f + 1], 0.0)
            put(f, value)
            put(FIELDS + f, answer)
            put(2 * FIELDS + f, jnp.where(even, layers[1, f, here], layers[0, f, here]))
        put(3 * FIELDS, jnp.where(even, bottom, roof))
    enters, leaves = wide[0, 0], wide[2, rows - 1]
    coefs = (
        jnp.where(upper, q, r * lift),
        jnp.where(upper, one, a),
        q * enters,
        a * enters,
        r * leaves,
        jnp.where(upper, enters, leaves),
        jnp.where(upper, one, lift),
    )
    out = zero
    for i, c in enumerate(coefs):
        out = jnp.where(lane == i * TILE + sub, c, out)
    out = jnp.broadcast_to(jnp.sum(out, axis=0, keepdims=True), tile)
    for v in range(tiles):
        packed[pl.ds(v * TILE * ROWS + ROWS - 1, TILE, stride=ROWS)] = out


def solve(got, base_in, out, base, entry):
    del base_in, base
    count = got.shape[0] // ROWS
    tile = (TILE, got.shape[1])
    sub, lane = row_of(tile), lane_of(tile)
    upper = sub < FIELDS
    zero = jnp.zeros(tile, f32)
    swap = lambda x: pltpu.roll(x, FIELDS, 0)

    def coefficient(k, i):
        row = jnp.broadcast_to(got[pl.ds(k * ROWS + ROWS - 1, 1)], tile)
        row = jnp.where(lane == i * TILE + sub, row, 0.0)
        return jnp.broadcast_to(jnp.sum(row, axis=1, keepdims=True), tile)

    twice = lambda x: jnp.concatenate([x, x], axis=0)
    e = zero
    for k in range(count):
        other = k + 1 if k % 2 else k - 1
        brought = zero
        if 0 <= other < count:
            layer = twice(got[pl.ds(other * ROWS + 2 * FIELDS, FIELDS)])
            brought = jnp.where(upper == (k % 2 == 0), got[pl.ds(k * ROWS + 3 * FIELDS, 1)] * layer, 0.0)
        both = got[pl.ds(k * ROWS, TILE)] + coefficient(k, 0) * brought + coefficient(k, 1) * swap(brought)
        entry[0, k] = both
        entry[1, k] = coefficient(k, 6) * brought
        out[k] = e
        e = jnp.where(upper, both, swap(both)) + coefficient(k, 2) * e
    b = zero
    for k in reversed(range(count)):
        both, e = entry[0, k], out[k]
        out[k] = coefficient(k, 5) * jnp.where(upper, e, b) + entry[1, k]
        b = jnp.where(upper, swap(both), both) + coefficient(k, 3) * e + coefficient(k, 4) * b


def finish(base, got, entry, resp, fix, out, start, stage, sems):
    rows, _, span, lanes = out.shape
    tiles = span // TILE
    sub = row_of((TILE, lanes))
    chunks = rows // STEP

    def store(c):
        here = pl.ds(c * STEP, STEP)
        return pltpu.make_async_copy(stage.at[here], out.at[here], sems.at[1, c])

    for f in range(FIELDS):
        for v in range(tiles):
            here = pl.ds(v * TILE, TILE)
            start[0, f, here] = got[pl.ds(v * TILE * TILE + f, TILE, stride=TILE)] + entry[0, f, here]
            start[1, f, here] = got[pl.ds(v * TILE * TILE + FIELDS + f, TILE, stride=TILE)] + entry[1, f, here]

    def body(c, carry):
        for f in range(FIELDS):
            u = [start[0, f, pl.ds(v * TILE, TILE)] for v in range(tiles)]
            w = [start[1, f, pl.ds(v * TILE, TILE)] for v in range(tiles)]
            for i in range(STEP):
                j = c * STEP + i
                a, r = resp[j, pl.ds(f, 1)], resp[j, pl.ds(FIELDS + f, 1)]
                for v in range(tiles):
                    here = pl.ds(v * TILE, TILE)
                    x = base[j, f, here] + a * u[v] + r * w[v]
                    if v == 0:
                        x = x + jnp.where(sub == 0, fix[j, pl.ds(f, 1)], 0.0)
                    if v == tiles - 1:
                        x = x + jnp.where(sub == TILE - 1, fix[j, pl.ds(FIELDS + f, 1)], 0.0)
                    stage[j, f, here] = x
        store(c).start()
        return carry

    lax.fori_loop(0, chunks, body, 0)
    for c in range(chunks):
        store(c).wait()


def params(mib):
    return pltpu.CompilerParams(vmem_limit_bytes=mib << 20)


def on_device(fields, kappa, fwd, piv, bwd):
    rows, nf, span, lanes = fields.shape
    shape = lambda *s: jax.ShapeDtypeStruct(s, f32)
    vmem = lambda *s: pltpu.VMEM(s, f32)
    in_vmem = lambda x: pltpu.with_memory_space_constraint(x, pltpu.VMEM)
    in_hbm = lambda x: pltpu.with_memory_space_constraint(x, pltpu.HBM)
    count = lax.axis_size(GY)
    around = lax.axis_size(GZ)
    pairs = lambda n, first: [(i, i + 1) for i in range(first, n - 1, 2)]
    both = lambda ends: ends + [(b, a) for a, b in ends]
    side = lax.axis_index("c").astype(jnp.int32).reshape(1)
    odd = (lax.axis_index("z") & 1).astype(jnp.int32).reshape(1)
    fwd, piv, bwd = fwd.T, piv.T, bwd.T
    fields, kappa = in_hbm(fields), in_hbm(kappa)
    chunks = rows // STEP
    weight, wide, inner, outer, near = pl.pallas_call(
        collect,
        out_shape=(
            vmem(rows, span, lanes),
            vmem(3, rows, TILE, lanes),
            vmem(rows, nf, 1, lanes),
            vmem(rows, nf, 1, lanes),
            vmem(nf, span, lanes),
        ),
        in_specs=[SMEM, SMEM] + [HBM] * 5,
        out_specs=(VMEM,) * 5,
        scratch_shapes=[pltpu.VMEM((3, nf, rows), f32), pltpu.SemaphoreType.DMA((7,))],
        compiler_params=params(4),
        name="collect",
    )(side, odd, *map(in_hbm, (fields, kappa, fwd, piv, bwd)))
    outer = lax.ppermute(outer, GZ, both(pairs(around, 1) + [(around - 1, 0)]))
    near = lax.ppermute(near, GY, both(pairs(count, 0)))
    inner = lax.ppermute(inner, GZ, both(pairs(around, 0)))
    block = in_vmem(fields), in_vmem(weight), in_vmem(wide)
    base, last, layers, first = pl.pallas_call(
        sweeps,
        out_shape=(
            vmem(rows, nf, span, lanes),
            vmem(nf, span, lanes),
            vmem(2, nf, span, lanes),
            vmem(nf, span, lanes),
        ),
        in_specs=[VMEM] * 3,
        out_specs=(VMEM,) * 4,
        scratch_shapes=[pltpu.VMEM((LONG, nf, span, lanes), f32)],
        compiler_params=params(4),
        cost_estimate=pl.CostEstimate(flops=20 * fields.size, bytes_accessed=4 * fields.size, transcendentals=0),
        name="sweeps",
    )(*block)

    base, fix, packed, resp, entry = pl.pallas_call(
        edges,
        out_shape=(
            vmem(rows, nf, span, lanes),
            shape(rows, TILE, lanes),
            shape(span * ROWS, lanes),
            shape(rows, TILE, lanes),
            shape(2, nf, span, lanes),
        ),
        in_specs=[SMEM, SMEM] + [VMEM] * 9,
        out_specs=(VMEM,) * 5,
        input_output_aliases={2: 0},
        compiler_params=params(4),
        name="edges",
    )(side, odd, in_vmem(base), last, first, in_vmem(weight), inner, outer, near, layers, in_vmem(wide))

    got = lax.all_to_all(packed.reshape(count, ROWS, 1, lanes), GY, 0, 0)
    out, base = pl.pallas_call(
        solve,
        out_shape=(shape(count, TILE, lanes), pltpu.VMEM((rows, nf, span, lanes), f32)),
        in_specs=[VMEM, VMEM],
        out_specs=(VMEM, VMEM),
        input_output_aliases={1: 1},
        scratch_shapes=[pltpu.VMEM((2, count, TILE, lanes), f32)],
        compiler_params=params(4),
        name="solve",
    )(got.reshape(count * ROWS, lanes), in_vmem(base))
    back = lax.all_to_all(out, GY, 0, 0)
    return pl.pallas_call(
        finish,
        out_shape=shape(rows, nf, span, lanes),
        in_specs=[VMEM] * 5,
        out_specs=HBM,
        scratch_shapes=[
            pltpu.VMEM((2, nf, span, lanes), f32),
            pltpu.VMEM((rows, nf, span, lanes), f32),
            pltpu.SemaphoreType.DMA((2, chunks)),
        ],
        compiler_params=params(16),
        name="finish",
    )(in_vmem(base), back.reshape(count * TILE, lanes), entry, resp, fix)


def solution(mesh):
    nz = 8 if mesh.shape["gy"] % 8 == 0 else 1
    split = Mesh(mesh.devices.reshape(-1, nz, mesh.shape["gz"] // 2, 2), GY + GZ)
    placed = (P(GY, None, GZ, None), P(GY, GZ, None), P(GY, None), P(GY, None), P(GY, None))
    return jax.shard_map(
        on_device, mesh=split, in_specs=placed, out_specs=P(GY, None, GZ, None), check_vma=False
    )
```

```python
import jax
import jax.numpy as jnp
from jax import lax
from jax.experimental import pallas as pl
from jax.experimental.pallas import tpu as pltpu
from jax.sharding import Mesh
from jax.sharding import PartitionSpec as P

GY = ("y", "z")
GZ = ("x", "c")
FIELDS = 4
TILE = 8
LONG = 16
STEP = 8
ROWS = 3 * FIELDS + 2

VMEM = pl.BlockSpec(memory_space=pltpu.VMEM)
SMEM = pl.BlockSpec(memory_space=pltpu.SMEM)
HBM = pl.BlockSpec(memory_space=pltpu.HBM)
f32 = jnp.float32


def row_of(shape):
    return lax.broadcasted_iota(jnp.int32, shape, 0)


def lane_of(shape):
    return lax.broadcasted_iota(jnp.int32, shape, 1)


def collect(side, odd, fields, kappa, fwd, piv, bwd, weight, wide, inner, outer, near, narrow, sems):
    rows, _, span, lanes = fields.shape
    z_near = jnp.where(side[0] == 0, span - 1, 0)
    copies = [
        pltpu.make_async_copy(fields.at[:, :, pl.ds(span - 1 - z_near, 1)], outer, sems.at[0]),
        pltpu.make_async_copy(fields.at[:, :, pl.ds(z_near, 1)], inner, sems.at[1]),
        pltpu.make_async_copy(fields.at[jnp.where(odd[0] == 0, rows - 1, 0)], near, sems.at[2]),
        pltpu.make_async_copy(kappa, weight, sems.at[3]),
    ]
    small = [pltpu.make_async_copy(ref, narrow.at[i], sems.at[4 + i]) for i, ref in enumerate((fwd, piv, bwd))]
    for copy in small + copies:
        copy.start()
    for copy in small:
        copy.wait()
    for i in range(3):
        x = narrow[i]
        x = jnp.concatenate([x, x], axis=0)
        for j in range(rows):
            wide[i, j] = jnp.broadcast_to(x[:, j : j + 1], (TILE, lanes))
    for copy in copies:
        copy.wait()


def forward(fields, weight, wide, sweep, state, layers, fresh):
    rows, _, span, lanes = sweep.shape
    tiles = span // TILE
    tile = (TILE, lanes)
    at = lambda v: pl.ds(v * TILE, TILE)
    sub = row_of(tile)
    total = rows // LONG
    layers[0] = fields[rows - 1]
    layers[1] = fields[0]

    def beside(j, f, v, x):
        if v == 0:
            low = jnp.where(sub == 0, 0.0, pltpu.roll(x, 1, 0))
        else:
            low = fields[j, f, pl.ds(v * TILE - 1, TILE)]
        if v == tiles - 1:
            return low + jnp.where(sub == TILE - 1, 0.0, pltpu.roll(x, TILE - 1, 0))
        return low + fields[j, f, pl.ds(v * TILE + 1, TILE)]

    def update(c):
        above_first = jnp.where(jnp.broadcast_to(c, tile) > 0, 1.0, 0.0)
        below_last = jnp.where(jnp.broadcast_to(c, tile) < total - 1, 1.0, 0.0)
        for v in range(tiles):
            under = [fields[jnp.maximum(c * LONG - 1, 0), f, at(v)] * above_first for f in range(FIELDS)]
            here = [fields[c * LONG, f, at(v)] for f in range(FIELDS)]
            for i in range(LONG):
                j = c * LONG + i
                k = weight[j, at(v)]
                own = 1.0 - 6.0 * k
                half = 0.5 * here[0]
                for f in range(FIELDS):
                    x = here[f]
                    if i < LONG - 1:
                        over = fields[j + 1, f, at(v)]
                    else:
                        over = fields[jnp.minimum(j + 1, rows - 1), f, at(v)] * below_last
                    around = beside(j, f, v, x)
                    around = around + (pltpu.roll(x, 1, 1) + pltpu.roll(x, lanes - 1, 1))
                    around = around + (under[f] + over)
                    new = own * x + k * around
                    if f == 2:
                        new = new + half
                    fresh[i, f, at(v)] = new
                    under[f], here[f] = x, over

    def advance(c, carry):
        carry = list(carry)
        for i in range(LONG):
            j = c * LONG + i
            for f in range(FIELDS):
                m = wide[0, j, pl.ds(f, 1)]
                for v in range(tiles):
                    k = f * tiles + v
                    carry[k] = fresh[i, f, at(v)] + m * carry[k]
                    sweep[j, f, at(v)] = carry[k]
        return tuple(carry)

    def both(c, carry):
        carry = advance(c - 1, carry)
        update(c)
        return carry

    update(0)
    carry = lax.fori_loop(1, total, both, (jnp.zeros(tile, f32),) * (FIELDS * tiles))
    carry = advance(total - 1, carry)
    for f in range(FIELDS):
        for v in range(tiles):
            state[f, at(v)] = carry[f * tiles + v]


def backward(wide, sweep, base, first):
    rows, _, span, lanes = base.shape
    tiles = span // TILE
    at = lambda v: pl.ds(v * TILE, TILE)

    def body(t, state):
        state = list(state)
        for i in range(2 * STEP):
            j = rows - 1 - (t * 2 * STEP + i)
            for f in range(FIELDS):
                p, m = wide[1, j, pl.ds(f, 1)], wide[2, j, pl.ds(f, 1)]
                for v in range(tiles):
                    k = f * tiles + v
                    state[k] = p * base[j, f, at(v)] + m * state[k]
                    base[j, f, at(v)] = state[k]
        return tuple(state)

    start = (jnp.zeros((TILE, lanes), f32),) * (FIELDS * tiles)
    state = lax.fori_loop(0, rows // (2 * STEP), body, start)
    for f in range(FIELDS):
        for v in range(tiles):
            first[f, at(v)] = state[f * tiles + v]


def sweeps(fields, weight, wide, base, last, layers, first, fresh):
    forward(fields, weight, wide, base, last, layers, fresh)
    backward(wide, None, base, first)


def edges(side, odd, base_in, last, first, kappa, inner, outer, near, layers, wide, base, fix, packed, resp, entry):
    del base_in, base
    nf, span, lanes = last.shape
    rows = fix.shape[0]
    tiles = span // TILE
    tile = (TILE, lanes)
    sub, lane = row_of(tile), lane_of(tile)
    low, high = sub == 0, sub == TILE - 1
    upper = sub < FIELDS
    flip = jnp.broadcast_to(side[0], tile) == 1
    even = jnp.broadcast_to(odd[0], tile) == 0
    zero, one = jnp.zeros(tile, f32), jnp.ones(tile, f32)
    twice = lambda x: jnp.concatenate([x, x], axis=0)

    def added(j):
        x = jnp.where(upper == flip, twice(inner[j, :, 0]), twice(outer[j, :, 0]))
        return jnp.where(upper, kappa[j, pl.ds(0, 1)], kappa[j, pl.ds(span - 1, 1)]) * x

    state, q = zero, one
    for j in range(0, rows, 2):
        x0, x1, m0, m1 = added(j), added(j + 1), wide[0, j], wide[0, j + 1]
        fix[j] = x0 + m0 * state
        state = (x1 + m1 * x0) + (m1 * m0) * state
        fix[j + 1] = state
        n0 = m0 if j else one
        resp[j] = n0 * q
        q = (m1 * n0) * q
        resp[j + 1] = q
    top, a, r = zero, zero, one
    for j in reversed(range(1, rows, 2)):
        p1, m1, p0, m0 = wide[1, j], wide[2, j], wide[1, j - 1], wide[2, j - 1]
        f1, f0, a1, a0 = p1 * fix[j], p0 * fix[j - 1], p1 * resp[j], p0 * resp[j - 1]
        fix[j] = f1 + m1 * top
        top = (f0 + m0 * f1) + (m0 * m1) * top
        fix[j - 1] = top
        n1 = m1 if j < rows - 1 else one
        resp[j] = jnp.where(upper, a1 + m1 * a, n1 * r)
        a = (a0 + m0 * a1) + (m0 * m1) * a
        r = (m0 * n1) * r
        resp[j - 1] = jnp.where(upper, a, r)

    lift = wide[1, rows - 1]
    by_value, by_answer = jnp.where(even, one, q), jnp.where(even, r * lift, a)
    for v in range(tiles):
        here = pl.ds(v * TILE, TILE)
        put = lambda i, x: packed.__setitem__(pl.ds(v * TILE * ROWS + i, TILE, stride=ROWS), x)
        bottom, roof = kappa[0, here], kappa[rows - 1, here]
        for f in range(FIELDS):
            brought = jnp.where(even, roof, bottom) * near[f, here]
            entry[0, f, here] = jnp.where(even, 0.0, brought)
            entry[1, f, here] = jnp.where(even, lift[f : f + 1] * brought, 0.0)
            value = last[f, here] + by_value[f : f + 1] * brought
            answer = first[f, here] + by_answer[f : f + 1] * brought
            if v == 0:
                value = value + jnp.where(low, state[f : f + 1], 0.0)
                answer = answer + jnp.where(low, top[f : f + 1], 0.0)
            if v == tiles - 1:
                value = value + jnp.where(high, state[FIELDS + f : FIELDS + f + 1], 0.0)
                answer = answer + jnp.where(high, top[FIELDS + f : FIELDS + f + 1], 0.0)
            put(f, value)
            put(FIELDS + f, answer)
            put(2 * FIELDS + f, jnp.where(even, layers[1, f, here], layers[0, f, here]))
        put(3 * FIELDS, jnp.where(even, bottom, roof))
    enters, leaves = wide[0, 0], wide[2, rows - 1]
    coefs = (
        jnp.where(upper, q, r * lift),
        jnp.where(upper, one, a),
        q * enters,
        a * enters,
        r * leaves,
        jnp.where(upper, enters, leaves),
        jnp.where(upper, one, lift),
    )
    out = zero
    for i, c in enumerate(coefs):
        out = jnp.where(lane == i * TILE + sub, c, out)
    out = jnp.broadcast_to(jnp.sum(out, axis=0, keepdims=True), tile)
    for v in range(tiles):
        packed[pl.ds(v * TILE * ROWS + ROWS - 1, TILE, stride=ROWS)] = out


def solve(got, base_in, out, base, entry):
    del base_in, base
    count = got.shape[0] // ROWS
    tile = (TILE, got.shape[1])
    sub, lane = row_of(tile), lane_of(tile)
    upper = sub < FIELDS
    zero = jnp.zeros(tile, f32)
    swap = lambda x: pltpu.roll(x, FIELDS, 0)

    def coefficient(k, i):
        row = jnp.broadcast_to(got[pl.ds(k * ROWS + ROWS - 1, 1)], tile)
        row = jnp.where(lane == i * TILE + sub, row, 0.0)
        return jnp.broadcast_to(jnp.sum(row, axis=1, keepdims=True), tile)

    twice = lambda x: jnp.concatenate([x, x], axis=0)
    e = zero
    for k in range(count):
        other = k + 1 if k % 2 else k - 1
        brought = zero
        if 0 <= other < count:
            layer = twice(got[pl.ds(other * ROWS + 2 * FIELDS, FIELDS)])
            brought = jnp.where(upper == (k % 2 == 0), got[pl.ds(k * ROWS + 3 * FIELDS, 1)] * layer, 0.0)
        both = got[pl.ds(k * ROWS, TILE)] + coefficient(k, 0) * brought + coefficient(k, 1) * swap(brought)
        entry[0, k] = both
        entry[1, k] = coefficient(k, 6) * brought
        out[k] = e
        e = jnp.where(upper, both, swap(both)) + coefficient(k, 2) * e
    b = zero
    for k in reversed(range(count)):
        both, e = entry[0, k], out[k]
        out[k] = coefficient(k, 5) * jnp.where(upper, e, b) + entry[1, k]
        b = jnp.where(upper, swap(both), both) + coefficient(k, 3) * e + coefficient(k, 4) * b


def finish(base, got, entry, resp, fix, out, start, stage, sems):
    rows, _, span, lanes = out.shape
    tiles = span // TILE
    sub = row_of((TILE, lanes))
    chunks = rows // STEP

    def store(c):
        here = pl.ds(c * STEP, STEP)
        return pltpu.make_async_copy(stage.at[here], out.at[here], sems.at[1, c])

    for f in range(FIELDS):
        for v in range(tiles):
            here = pl.ds(v * TILE, TILE)
            start[0, f, here] = got[pl.ds(v * TILE * TILE + f, TILE, stride=TILE)] + entry[0, f, here]
            start[1, f, here] = got[pl.ds(v * TILE * TILE + FIELDS + f, TILE, stride=TILE)] + entry[1, f, here]

    def body(c, carry):
        for f in range(FIELDS):
            u = [start[0, f, pl.ds(v * TILE, TILE)] for v in range(tiles)]
            w = [start[1, f, pl.ds(v * TILE, TILE)] for v in range(tiles)]
            for i in range(STEP):
                j = c * STEP + i
                a, r = resp[j, pl.ds(f, 1)], resp[j, pl.ds(FIELDS + f, 1)]
                for v in range(tiles):
                    here = pl.ds(v * TILE, TILE)
                    x = base[j, f, here] + a * u[v] + r * w[v]
                    if v == 0:
                        x = x + jnp.where(sub == 0, fix[j, pl.ds(f, 1)], 0.0)
                    if v == tiles - 1:
                        x = x + jnp.where(sub == TILE - 1, fix[j, pl.ds(FIELDS + f, 1)], 0.0)
                    stage[j, f, here] = x
        store(c).start()
        return carry

    lax.fori_loop(0, chunks, body, 0)
    for c in range(chunks):
        store(c).wait()


def params(mib):
    return pltpu.CompilerParams(vmem_limit_bytes=mib << 20)


def on_device(fields, kappa, fwd, piv, bwd):
    rows, nf, span, lanes = fields.shape
    shape = lambda *s: jax.ShapeDtypeStruct(s, f32)
    vmem = lambda *s: pltpu.VMEM(s, f32)
    in_vmem = lambda x: pltpu.with_memory_space_constraint(x, pltpu.VMEM)
    in_hbm = lambda x: pltpu.with_memory_space_constraint(x, pltpu.HBM)
    count = lax.axis_size(GY)
    around = lax.axis_size(GZ)
    pairs = lambda n, first: [(i, i + 1) for i in range(first, n - 1, 2)]
    both = lambda ends: ends + [(b, a) for a, b in ends]
    side = lax.axis_index("c").astype(jnp.int32).reshape(1)
    odd = (lax.axis_index("z") & 1).astype(jnp.int32).reshape(1)
    fwd, piv, bwd = fwd.T, piv.T, bwd.T
    fields, kappa = in_hbm(fields), in_hbm(kappa)
    chunks = rows // STEP
    weight, wide, inner, outer, near = pl.pallas_call(
        collect,
        out_shape=(
            vmem(rows, span, lanes),
            vmem(3, rows, TILE, lanes),
            vmem(rows, nf, 1, lanes),
            vmem(rows, nf, 1, lanes),
            vmem(nf, span, lanes),
        ),
        in_specs=[SMEM, SMEM] + [HBM] * 5,
        out_specs=(VMEM,) * 5,
        scratch_shapes=[pltpu.VMEM((3, nf, rows), f32), pltpu.SemaphoreType.DMA((7,))],
        compiler_params=params(4),
        name="collect",
    )(side, odd, *map(in_hbm, (fields, kappa, fwd, piv, bwd)))
    outer = lax.ppermute(outer, GZ, both(pairs(around, 1) + [(around - 1, 0)]))
    near = lax.ppermute(near, GY, both(pairs(count, 0)))
    inner = lax.ppermute(inner, GZ, both(pairs(around, 0)))
    block = in_vmem(fields), in_vmem(weight), in_vmem(wide)
    base, last, layers, first = pl.pallas_call(
        sweeps,
        out_shape=(
            vmem(rows, nf, span, lanes),
            vmem(nf, span, lanes),
            vmem(2, nf, span, lanes),
            vmem(nf, span, lanes),
        ),
        in_specs=[VMEM] * 3,
        out_specs=(VMEM,) * 4,
        scratch_shapes=[pltpu.VMEM((LONG, nf, span, lanes), f32)],
        compiler_params=params(4),
        cost_estimate=pl.CostEstimate(flops=20 * fields.size, bytes_accessed=4 * fields.size, transcendentals=0),
        name="sweeps",
    )(*block)

    base, fix, packed, resp, entry = pl.pallas_call(
        edges,
        out_shape=(
            vmem(rows, nf, span, lanes),
            shape(rows, TILE, lanes),
            shape(span * ROWS, lanes),
            shape(rows, TILE, lanes),
            shape(2, nf, span, lanes),
        ),
        in_specs=[SMEM, SMEM] + [VMEM] * 9,
        out_specs=(VMEM,) * 5,
        input_output_aliases={2: 0},
        compiler_params=params(4),
        name="edges",
    )(side, odd, in_vmem(base), last, first, in_vmem(weight), inner, outer, near, layers, in_vmem(wide))

    got = lax.all_to_all(packed.reshape(count, ROWS, 1, lanes), GY, 0, 0)
    out, base = pl.pallas_call(
        solve,
        out_shape=(shape(count, TILE, lanes), pltpu.VMEM((rows, nf, span, lanes), f32)),
        in_specs=[VMEM, VMEM],
        out_specs=(VMEM, VMEM),
        input_output_aliases={1: 1},
        scratch_shapes=[pltpu.VMEM((2, count, TILE, lanes), f32)],
        compiler_params=params(4),
        name="solve",
    )(got.reshape(count * ROWS, lanes), in_vmem(base))
    back = lax.all_to_all(out, GY, 0, 0)
    return pl.pallas_call(
        finish,
        out_shape=shape(rows, nf, span, lanes),
        in_specs=[VMEM] * 5,
        out_specs=HBM,
        scratch_shapes=[
            pltpu.VMEM((2, nf, span, lanes), f32),
            pltpu.VMEM((rows, nf, span, lanes), f32),
            pltpu.SemaphoreType.DMA((2, chunks)),
        ],
        compiler_params=params(16),
        name="finish",
    )(in_vmem(base), back.reshape(count * TILE, lanes), entry, resp, fix)


def solution(mesh):
    nz = 8 if mesh.shape["gy"] % 8 == 0 else 1
    split = Mesh(mesh.devices.reshape(-1, nz, mesh.shape["gz"] // 2, 2), GY + GZ)
    placed = (P(GY, None, GZ, None), P(GY, GZ, None), P(GY, None), P(GY, None), P(GY, None))
    return jax.shard_map(
        on_device, mesh=split, in_specs=placed, out_specs=P(GY, None, GZ, None), check_vma=False
    )
```
